32 devices in a mesh: task: 4 (over y, x), feat: 8 (over z, core).
Axes of the slice: x: 2, y: 2, z: 4, core: 2. Of those that a mesh axis runs over, the one named last changes fastest.
Arguments:
- layer_input: bfloat16 [8, 16, 512, 512], P('task', 'feat'), may hold values from -6 to 6
- cotangent: bfloat16 [8, 16, 512, 512], P('task', 'feat'), may hold values from -6 to 6
- sample_len: int32 [8], P('task'), may hold values from 50 to 512, as said below
- feat_count: int32 [8], P('task'), may hold values from 4 to 16, as said below
- ln1_gain: float32 [512], replicated, may hold values from 0.5 to 1.5
- ln1_bias: float32 [512], replicated, may hold values from -2 to 2
- qkv1_weight: bfloat16 [512, 1536], replicated, may hold values from -0.375 to 0.375
- out1_weight: bfloat16 [512, 512], replicated, may hold values from -1 to 1
- ln2_gain: float32 [512], replicated, may hold values from 0.5 to 1.5
- ln2_bias: float32 [512], replicated, may hold values from -2 to 2
- qkv2_weight: bfloat16 [512, 1536], replicated, may hold values from -0.375 to 0.375
- out2_weight: bfloat16 [512, 512], replicated, may hold values from -0.75 to 0.75
- ln3_gain: float32 [512], replicated, may hold values from 0.5 to 1.5
- ln3_bias: float32 [512], replicated, may hold values from -2 to 2
- up_weight: bfloat16 [512, 2048], replicated, may hold values from -0.25 to 0.25
- up_bias: float32 [2048], replicated, may hold values from -3 to 3
- down_weight: bfloat16 [2048, 512], replicated, may hold values from -0.125 to 0.125
- down_bias: float32 [512], replicated, may hold values from -3 to 3
Outputs:
- layer_output: bfloat16 [8, 16, 512, 512], P('task', 'feat')
- input_grad: bfloat16 [8, 16, 512, 512], P('task', 'feat')
- ln1_gain_grad: float32 [512], P('feat')
- ln1_bias_grad: float32 [512], P('feat')
- qkv1_weight_grad: float32 [512, 1536], P('feat')
- out1_weight_grad: float32 [512, 512], P('feat')
- ln2_gain_grad: float32 [512], P('feat')
- ln2_bias_grad: float32 [512], P('feat')
- qkv2_weight_grad: float32 [512, 1536], P('feat')
- out2_weight_grad: float32 [512, 512], P('feat')
- ln3_gain_grad: float32 [512], P('feat')
- ln3_bias_grad: float32 [512], P('feat')
- up_weight_grad: float32 [512, 2048], P('feat')
- up_bias_grad: float32 [2048], P('feat')
- down_weight_grad: float32 [2048, 512], P('feat')
- down_bias_grad: float32 [512], P('feat')
The draws below stay inside these ranges and needn't reach their ends.
Inputs may be any that keep to these rules, and one draw needn't show every extreme that they name: `sample_len`: in every block of 2 consecutive tasks one task has all 512 samples. `feat_count`: in every block of 2 consecutive tasks one task has all 16 features.
All inputs are finite; a program needn't handle non-finite values.
Results may differ from the reference program's by a relative error of at most 0.024.
Values may be sent and summed in bfloat16 or wider, within the bound.
No kernel may reach another device: no remote copies, remote signals or barrier semaphores. Data moves between devices by JAX's collectives and lax.ppermute only.
A program may use at most 256 MiB of HBM per device.

```python
import jax
import jax.numpy as jnp
from jax import lax

D = 512
HEADS = 8
HEAD_DIM = 64
FF = 2048
SAMPLES = 512
TASK_DEV = 2
TASKS = 8
FEATS = 16


def blocks_with_full(key, lowest, highest):
    counts = jax.random.randint(jax.random.fold_in(key, 11), (TASKS,), lowest, highest + 1)
    picked = jax.random.randint(jax.random.fold_in(key, 12), (TASKS // TASK_DEV,), 0, TASK_DEV)
    member = jnp.arange(TASKS) % TASK_DEV
    chosen = member == jnp.repeat(picked, TASK_DEV)
    return jnp.where(chosen, highest, counts).astype(jnp.int32)


def draw_sample_len(key, part):
    return blocks_with_full(key, max(1, SAMPLES * 50 // 512), SAMPLES)


def draw_feat_count(key, part):
    return blocks_with_full(key, max(1, FEATS // 4), FEATS)


def shard_levels(own_key, extent, split, least, top_value):
    def one(dim, shards_of):
        draws = jax.random.uniform(jax.random.fold_in(jax.random.fold_in(own_key, 6), dim), (shards_of,), jnp.float32, least / len(split), top_value / len(split))
        return jnp.repeat(jnp.exp(draws), extent[dim] // shards_of).reshape((-1,) + (1,) * (len(extent) - dim - 1))

    loudness = one(*split[0])
    for cut in split[1:]:
        loudness = loudness * one(*cut)
    return loudness


def noise(stream_key, shape, deviation, most, shards=(), kind=jnp.bfloat16):
    entries = jax.random.normal(stream_key, shape, jnp.float32) * deviation
    if len(shards) > 0:
        entries = shard_levels(stream_key, shape, shards, -0.22, 0.18) * entries
    return jnp.clip(entries, min=-most, max=most).astype(kind)


def setup_inputs(seed: int = 0) -> dict:
    key_list = jax.random.split(jax.random.key(seed), 19)
    return {
        "layer_input": noise(key_list[0], (TASKS, FEATS, SAMPLES, D), 1.0, 6.0, ((0, 4), (1, 8))),
        "cotangent": noise(key_list[1], (TASKS, FEATS, SAMPLES, D), 1.0, 6.0, ((0, 4), (1, 8))),
        "sample_len": draw_sample_len(jax.random.fold_in(key_list[18], 71), 0),
        "feat_count": draw_feat_count(jax.random.fold_in(key_list[18], 71), 0),
        "ln1_gain": jnp.clip(1.0 + 0.1 * jax.random.normal(key_list[4], (D,), jnp.float32), 0.5, 1.5),
        "ln1_bias": noise(key_list[5], (D,), 0.3, 2.0, (), jnp.float32),
        "qkv1_weight": noise(key_list[6], (D, 3 * D), (D // 2) ** -0.5, 0.375),
        "out1_weight": noise(key_list[7], (D, D), (D // 16) ** -0.5, 1.0),
        "ln2_gain": jnp.clip(1.0 + 0.1 * jax.random.normal(key_list[8], (D,), jnp.float32), 0.5, 1.5),
        "ln2_bias": noise(key_list[9], (D,), 0.3, 2.0, (), jnp.float32),
        "qkv2_weight": noise(key_list[10], (D, 3 * D), (D // 2) ** -0.5, 0.375),
        "out2_weight": noise(key_list[11], (D, D), (D // 8) ** -0.5, 0.75),
        "ln3_gain": jnp.clip(1.0 + 0.1 * jax.random.normal(key_list[12], (D,), jnp.float32), 0.5, 1.5),
        "ln3_bias": noise(key_list[13], (D,), 0.3, 2.0, (), jnp.float32),
        "up_weight": noise(key_list[14], (D, FF), D ** -0.5, 0.25),
        "up_bias": noise(key_list[15], (FF,), 0.5, 3.0, (), jnp.float32),
        "down_weight": noise(key_list[16], (FF, D), FF ** -0.5, 0.125),
        "down_bias": noise(key_list[17], (D,), 0.5, 3.0, (), jnp.float32),
    }


@jax.custom_vjp
def low(v):
    return lax.optimization_barrier(v.astype(jnp.bfloat16)).astype(jnp.float32)

@jax.custom_vjp
def low_back(v):
    return v

def low_keep(v):
    return (low(v), None)

def low_pass(kept, grad):
    return (grad,)

def back_keep(v):
    return (v, None)

def back_low(kept, grad):
    return (low(grad),)
low.defvjp(low_keep, low_pass)
low_back.defvjp(back_keep, back_low)
EPSILON = 1e-05

def normalize(hidden, factor, offset):
    average = lax.optimization_barrier(jnp.mean(hidden, axis=-1, keepdims=True))
    centred = hidden - average
    variance = lax.optimization_barrier(jnp.mean(centred * centred, axis=-1, keepdims=True))
    return centred * lax.rsqrt(variance + EPSILON) * factor + offset

def dense_product(left, right):
    return jnp.einsum('...d,de->...e', left, right, precision=lax.Precision.HIGHEST)

def attend_core(queries, keys_all, values_all, key_mask):
    raw_scores = jnp.einsum('bqhe,bkhe->bhqk', queries, keys_all, precision=lax.Precision.HIGHEST)
    scores = low_back(raw_scores * HEAD_DIM ** (-0.5))
    scores = jnp.where(key_mask, scores, -1e+30)
    row_max = lax.optimization_barrier(jnp.max(scores, axis=-1, keepdims=True))
    exp_terms = jnp.exp(scores - row_max)
    probabilities = low(exp_terms / lax.optimization_barrier(jnp.sum(exp_terms, axis=-1, keepdims=True)))
    return jnp.einsum('bhqk,bkhe->bqhe', probabilities, values_all, precision=lax.Precision.HIGHEST)

def branch(hidden, factor, offset, packed_weight, out_weight, key_mask, by_rows, rounded_grad):
    normed = low(normalize(hidden, factor, offset))
    if rounded_grad:
        normed = low_back(normed)
    packed = low_back(low(dense_product(normed, packed_weight)))
    split_heads = packed.reshape(packed.shape[:-1] + (3, HEADS, HEAD_DIM))
    queries = split_heads[..., 0, :, :]
    keys_all = split_heads[..., 1, :, :]
    values_all = split_heads[..., 2, :, :]
    if by_rows:

        def one_row(members):
            return attend_core(members[0][None], members[1][None], members[2][None], key_mask)[0]
        head_rows = lax.map(jax.checkpoint(one_row), (queries, keys_all, values_all))
    else:
        head_rows = attend_core(queries, keys_all, values_all, key_mask)
    head_rows = low_back(low(head_rows.reshape(hidden.shape)))
    return low_back(dense_product(head_rows, out_weight))

def task_layer(inputs, length, feature_count, params):
    gain_one, shift_one, packed_one, project_one, gain_two, shift_two, packed_two, project_two, gain_three, shift_three, up_matrix, up_shift, down_matrix, down_shift = params
    sample_keep = jnp.arange(SAMPLES) < length
    feat_keep = jnp.arange(FEATS) < feature_count
    middle_one = inputs + branch(inputs, gain_one, shift_one, packed_one, project_one, sample_keep, True, False)
    swapped = jnp.swapaxes(middle_one, 0, 1)
    feature_branch = branch(swapped, gain_two, shift_two, packed_two, project_two, feat_keep, False, True)
    middle_two = middle_one + jnp.swapaxes(feature_branch, 0, 1)
    normed_three = low(normalize(middle_two, gain_three, shift_three))
    preact = low_back(dense_product(normed_three, up_matrix) + up_shift)
    activated = low(jax.nn.gelu(preact, approximate=False))
    return middle_two + low_back(dense_product(activated, down_matrix) + down_shift)

def reference(layer_input, cotangent, sample_len, feat_count, ln1_gain, ln1_bias, qkv1_weight, out1_weight, ln2_gain, ln2_bias, qkv2_weight, out2_weight, ln3_gain, ln3_bias, up_weight, up_bias, down_weight, down_bias):
    params = (ln1_gain.astype(jnp.float32), ln1_bias.astype(jnp.float32), qkv1_weight.astype(jnp.float32), out1_weight.astype(jnp.float32), ln2_gain.astype(jnp.float32), ln2_bias.astype(jnp.float32), qkv2_weight.astype(jnp.float32), out2_weight.astype(jnp.float32), ln3_gain.astype(jnp.float32), ln3_bias.astype(jnp.float32), up_weight.astype(jnp.float32), up_bias.astype(jnp.float32), down_weight.astype(jnp.float32), down_bias.astype(jnp.float32))

    def forward(inputs, weights):

        def one_task(members):
            return task_layer(members[0], members[1], members[2], weights)
        return lax.map(jax.checkpoint(one_task), (inputs, sample_len, feat_count))
    result, pullback = jax.vjp(forward, layer_input.astype(jnp.float32), params)
    grad_inputs, grad_params = pullback(cotangent.astype(jnp.float32))
    return (result.astype(jnp.bfloat16), grad_inputs.astype(jnp.bfloat16), grad_params[0], grad_params[1], grad_params[2], grad_params[3], grad_params[4], grad_params[5], grad_params[6], grad_params[7], grad_params[8], grad_params[9], grad_params[10], grad_params[11], grad_params[12], grad_params[13])
```

```python
import math
from functools import partial
import jax, jax.numpy as jnp
from jax import lax
from jax.experimental import pallas as pl
from jax.experimental.pallas import tpu as pltpu
BF=jnp.bfloat16; F32=jnp.float32
EPS=1e-5
LOG2E=1.4426950408889634
QS=0.125*LOG2E

def dg(a,b,ca,cb):
    return lax.dot_general(a,b,(((ca,),(cb,)),((),())),preferred_element_type=F32)

def ln_stats(v):
    mean=jnp.mean(v,axis=-1,keepdims=True)
    c=v-mean
    var=jnp.mean(c*c,axis=-1,keepdims=True)
    return c, lax.rsqrt(var+EPS)

def split3(v):
    a=v.astype(BF); r=v-a.astype(F32)
    b=r.astype(BF); r=r-b.astype(F32)
    return a,b,r.astype(BF)

def pad_head(rows,u,aug):
    z=jnp.zeros_like(rows)
    return jnp.concatenate([rows,z,aug] if u==0 else [z,rows,aug],axis=0)

def lane_block(cols,n):
    lane=lax.broadcasted_iota(jnp.int32,(n,128),1)
    out=jnp.zeros((n,128),F32)
    for i,c in enumerate(cols):
        out=jnp.where(lane==i,c,out)
    return out.astype(BF)

def row_block(rows,n):
    sub=lax.broadcasted_iota(jnp.int32,(128,n),0)
    out=jnp.zeros((128,n),F32)
    for i,r in enumerate(rows):
        out=jnp.where(sub==i,r,out)
    return out.astype(BF)

def a_kernel(t, len_ref, x_ref, g_ref, b_ref, w_ref, wo_ref, mid_ref, qt_ref, k_ref, v_ref, ht_ref, l_ref):
    S,D=x_ref.shape[2:]
    x=x_ref[0,0].astype(F32)
    c,r=ln_stats(x)
    n1=(c*r*g_ref[...]+b_ref[...]).astype(BF)
    qt_ref[0]=(dg(w_ref[:,0:D],n1,0,1)*QS).astype(BF)
    k_ref[0]=dg(n1,w_ref[:,D:2*D],1,0).astype(BF)
    v_ref[0]=dg(n1,w_ref[:,2*D:3*D],1,0).astype(BF)
    n=len_ref[t]
    ks=lax.broadcasted_iota(jnp.int32,(S,1),0)
    bias=jnp.where(ks<n,0.0,-1e30)
    kb=lane_block([bias],S)
    qa=row_block([jnp.ones((1,S),F32)],S)
    ones=jnp.ones((16,S),BF)
    for p in range(D//128):
        kp=jnp.concatenate([k_ref[0,:,p*128:p*128+128],kb],axis=1)
        vt=v_ref[0,:,p*128:p*128+128].T
        for u in range(2):
            h=2*p+u
            q=pad_head(qt_ref[0,h*64:h*64+64,:],u,qa)
            s=dg(kp,q,1,0)
            m=jnp.max(s,axis=0,keepdims=True)
            e=jnp.exp2(s-m).astype(BF)
            va=jnp.concatenate([vt[u*64:u*64+64],ones],axis=0)
            o=dg(va,e,1,0)
            l=o[64:65]
            ht_ref[0,h*64:h*64+64,:]=(o[:64]*(1.0/l)).astype(BF)
            l_ref[0,h:h+1,:]=m+jnp.log2(l)
    mid=(x+dg(ht_ref[0],wo_ref[...],0,0)).astype(BF)
    nd=mid_ref.shape[0]
    for j in range(nd):
        mid_ref[j,0]=mid[j*(S//nd):(j+1)*(S//nd)]

def run_a(t, lens, x, g, b, w, wo, nd):
    T,F,S,D=x.shape
    grid_spec=pltpu.PrefetchScalarGridSpec(num_scalar_prefetch=1,grid=(F,),
        in_specs=[pl.BlockSpec((1,1,S,D),lambda f,s:(t,f,0,0)),
                  pl.BlockSpec((1,D),lambda f,s:(0,0)),pl.BlockSpec((1,D),lambda f,s:(0,0)),
                  pl.BlockSpec((D,3*D),lambda f,s:(0,0)),pl.BlockSpec((D,D),lambda f,s:(0,0))],
        out_specs=[pl.BlockSpec((nd,1,S//nd,D),lambda f,s:(0,f,0,0)),
                   pl.BlockSpec((1,D,S),lambda f,s:(f,0,0)),
                   pl.BlockSpec((1,S,D),lambda f,s:(f,0,0)),
                   pl.BlockSpec((1,S,D),lambda f,s:(f,0,0)),
                   pl.BlockSpec((1,D,S),lambda f,s:(f,0,0)),
                   pl.BlockSpec((1,D//64,S),lambda f,s:(f,0,0))])
    sd=jax.ShapeDtypeStruct
    return pl.pallas_call(partial(a_kernel,t),grid_spec=grid_spec,
        out_shape=[sd((nd,F,S//nd,D),BF),sd((F,D,S),BF),sd((F,S,D),BF),sd((F,S,D),BF),sd((F,D,S),BF),sd((F,D//64,S),F32)],
        compiler_params=pltpu.CompilerParams(vmem_limit_bytes=60<<20),name="fwd_samples",
        cost_estimate=pl.CostEstimate(flops=20_000_000_000,bytes_accessed=8<<20,transcendentals=4<<20))(lens,x,g.reshape(1,D),b.reshape(1,D),w,wo)

LN2=0.6931471805599453

def c_kernel(t, len_ref, x_ref, gm_ref, g_ref, b_ref, w_ref, wo_ref, qt_ref, k_ref, v_ref, ht_ref, l_ref, dx_ref, dw_ref, dwo_ref, dgb_ref, dot_ref, dpt_ref):
    S,D=x_ref.shape[2:]
    f=pl.program_id(0)
    x=x_ref[0,0].astype(F32)
    c,r=ln_stats(x)
    xh=c*r
    n1=(xh*g_ref[...]+b_ref[...]).astype(BF)
    nd=gm_ref.shape[0]
    s_in=jnp.concatenate([gm_ref[j,0] for j in range(nd)],axis=0)
    dot_ref[...]=dg(wo_ref[...],s_in,1,1).astype(BF)
    n=len_ref[t]
    ks=lax.broadcasted_iota(jnp.int32,(S,1),0)
    bias=jnp.where(ks<n,0.0,-1e30)
    one=jnp.ones((S,1),F32)
    kb=lane_block([bias,one,one,one],S)
    vb=lane_block([one,one,one],S)
    oner=jnp.ones((1,S),F32)
    for p in range(D//128):
        kp=jnp.concatenate([k_ref[0,:,p*128:p*128+128],kb],axis=1)
        vp=jnp.concatenate([v_ref[0,:,p*128:p*128+128],vb],axis=1)
        kt=k_ref[0,:,p*128:p*128+128].T
        for u in range(2):
            h=2*p+u
            hs=slice(h*64,h*64+64)
            L=l_ref[0,h:h+1,:]
            do=dot_ref[hs,:]
            dd=jnp.sum(do.astype(F32)*ht_ref[0,hs,:].astype(F32),axis=0,keepdims=True)
            l3=[-z.astype(F32) for z in split3(L)]
            d3=[-z.astype(F32) for z in split3(dd)]
            qa=row_block([oner]+l3,S)
            da=row_block(d3,S)
            s=dg(kp,pad_head(qt_ref[0,hs,:],u,qa),1,0)
            e=jnp.exp2(s)
            dp=dg(vp,pad_head(do,u,da),1,0)
            ds=(e*dp).astype(BF)
            e=e.astype(BF)
            dpt_ref[2*D+h*64:2*D+h*64+64,:]=dg(do,e,1,1).astype(BF)
            dpt_ref[D+h*64:D+h*64+64,:]=(dg(qt_ref[0,hs,:],ds,1,1)*LN2).astype(BF)
            dpt_ref[h*64:h*64+64,:]=(dg(kt[u*64:u*64+64],ds,1,0)*0.125).astype(BF)
    dw=dg(n1,dpt_ref[...],0,1)
    dwo=dg(ht_ref[0],s_in,1,0)
    dn=dg(dpt_ref[...],w_ref[...],0,1)
    dgain=jnp.sum(dn*xh,axis=0,keepdims=True)
    dbias=jnp.sum(dn,axis=0,keepdims=True)
    gd=dn*g_ref[...]
    dv=r*(gd-jnp.mean(gd,axis=-1,keepdims=True)-xh*jnp.mean(gd*xh,axis=-1,keepdims=True))
    dx_ref[0]=(s_in.astype(F32)+dv).astype(BF)
    @pl.when(f==0)
    def _():
        dw_ref[...]=dw; dwo_ref[...]=dwo
        dgb_ref[0:1]=dgain; dgb_ref[1:2]=dbias
    @pl.when(f>0)
    def _():
        dw_ref[...]+=dw; dwo_ref[...]+=dwo
        dgb_ref[0:1]+=dgain; dgb_ref[1:2]+=dbias

def run_c(t, lens, x, gm, g, b, w, wo, qt, k, v, ht, l):
    T,F,S,D=x.shape; nd=gm.shape[0]
    gs=pltpu.PrefetchScalarGridSpec(num_scalar_prefetch=1,grid=(F,),
        in_specs=[pl.BlockSpec((1,1,S,D),lambda f,s:(t,f,0,0)),
                  pl.BlockSpec((nd,1,S//nd,D),lambda f,s:(0,f,0,0)),
                  pl.BlockSpec((1,D),lambda f,s:(0,0)),pl.BlockSpec((1,D),lambda f,s:(0,0)),
                  pl.BlockSpec((D,3*D),lambda f,s:(0,0)),pl.BlockSpec((D,D),lambda f,s:(0,0)),
                   pl.BlockSpec((1,D,S),lambda f,s:(f,0,0)),
                   pl.BlockSpec((1,S,D),lambda f,s:(f,0,0)),
                   pl.BlockSpec((1,S,D),lambda f,s:(f,0,0)),
                   pl.BlockSpec((1,D,S),lambda f,s:(f,0,0)),
                   pl.BlockSpec((1,D//64,S),lambda f,s:(f,0,0))],
        out_specs=[pl.BlockSpec((1,S,D),lambda f,s:(f,0,0)),
                   pl.BlockSpec((D,3*D),lambda f,s:(0,0)),pl.BlockSpec((D,D),lambda f,s:(0,0)),
                   pl.BlockSpec((8,D),lambda f,s:(0,0))],
        scratch_shapes=[pltpu.VMEM((D,S),BF),pltpu.VMEM((3*D,S),BF)])
    sd=jax.ShapeDtypeStruct
    return pl.pallas_call(partial(c_kernel,t),grid_spec=gs,
        out_shape=[sd((F,S,D),BF),sd((D,3*D),F32),sd((D,D),F32),sd((8,D),F32)],
        compiler_params=pltpu.CompilerParams(vmem_limit_bytes=60<<20),name="bwd_samples",
        cost_estimate=pl.CostEstimate(flops=30_000_000_000,bytes_accessed=12<<20,transcendentals=4<<20))(lens,x,gm,g.reshape(1,D),b.reshape(1,D),w,wo,qt,k,v,ht,l)


def phi_pair(v):
    a=jnp.abs(v)
    t=1.0/(1.0+(0.3275911*0.7071067811865476)*a)
    e=jnp.exp2(v*v*(-0.5*LOG2E))
    y=t*(0.5*0.254829592+t*(0.5*-0.284496736+t*(0.5*1.421413741+t*(0.5*-1.453152027+t*(0.5*1.061405429)))))
    y=y*e
    return jnp.where(v<0,y,1.0-y), e*0.3989422804014327

def ln_back(dn,xh,r,gain):
    gd=dn*gain
    return r*(gd-jnp.mean(gd,axis=-1,keepdims=True)-xh*jnp.mean(gd*xh,axis=-1,keepdims=True))

def b_kernel(t, SB, cnt_ref, m_ref, cot_ref, g2_ref, b2_ref, w_ref, wo_ref, g3_ref, b3_ref, wu_ref, bu_ref, wd_ref, bd_ref,
             out_ref, gm_ref, dw_ref, dwo_ref, dwu_ref, dwd_ref, dv_ref, dbu_ref,
             n2_s, n3_s, r_s, ht_s, dpt_s, act_s, gp_s, cot_s, qt_s, k_s, v_s, e_s, dos_s):
    FA,_,D=m_ref.shape
    R=FA*SB
    H=D//64
    i=pl.program_id(0); last=pl.num_programs(0)-1
    rows=pl.ds(pl.multiple_of(i*R,R),R)
    m=m_ref[...].reshape(R,D).astype(F32)
    c,r2=ln_stats(m)
    xh2=c*r2
    n2=(xh2*g2_ref[...]+b2_ref[...]).astype(BF)
    n2_s[rows,:]=n2
    qt_s[...]=(dg(w_ref[:,0:D],n2,0,1)*QS).astype(BF)
    k_s[...]=dg(n2,w_ref[:,D:2*D],1,0).astype(BF)
    v_s[...]=dg(n2,w_ref[:,2*D:3*D],1,0).astype(BF)
    n=cnt_ref[t]
    krow=lax.broadcasted_iota(jnp.int32,(R,128),0)
    lane=lax.broadcasted_iota(jnp.int32,(R,128),1)
    kb=jnp.where(lane==0,jnp.where(krow//SB>=n,-1e30,0.0),jnp.where(lane-1==krow%SB,-1e30,0.0)).astype(BF)
    vb=jnp.where(lane<3,1.0,0.0).astype(BF)
    qcol=lax.broadcasted_iota(jnp.int32,(128,R),1)
    sub=lax.broadcasted_iota(jnp.int32,(128,R),0)
    qa=jnp.where((sub==0)|((sub<=SB)&(sub-1!=qcol%SB)),1.0,0.0).astype(BF)
    ones=jnp.ones((16,R),BF)
    rls=[]
    cols=pl.ds(pl.multiple_of(i*R,R),R)
    for p in range(D//128):
        kp=jnp.concatenate([k_s[:,p*128:p*128+128],kb],axis=1)
        vt=v_s[:,p*128:p*128+128].T
        for u in range(2):
            h=2*p+u
            s=dg(kp,pad_head(qt_s[h*64:h*64+64,:],u,qa),1,0)
            mx=jnp.max(s,axis=0,keepdims=True)
            e=jnp.exp2(s-mx).astype(BF)
            e_s[h]=e
            o=dg(jnp.concatenate([vt[u*64:u*64+64],ones],axis=0),e,1,0)
            rl=1.0/o[64:65]
            rls.append(rl)
            ht_s[h*64:h*64+64,cols]=(o[:64]*rl).astype(BF)
    m2=m+dg(ht_s[:,cols],wo_ref[...],0,0)
    c,r3=ln_stats(m2)
    xh3=c*r3
    n3=(xh3*g3_ref[...]+b3_ref[...]).astype(BF)
    n3_s[rows,:]=n3
    cot=cot_ref[...].reshape(R,D)
    cot_s[rows,:]=cot
    C=512
    dbu=[]
    for q in range(wu_ref.shape[1]//C):
        cs=slice(q*C,q*C+C)
        pre=dg(n3,wu_ref[:,cs],1,0)+bu_ref[:,cs]
        P,ph=phi_pair(pre)
        act_s[rows,cs]=(pre*P).astype(BF)
        gp=((P+pre*ph)*dg(cot,wd_ref[cs,:],1,1)).astype(BF)
        gp_s[rows,cs]=gp
        dbu.append(jnp.sum(gp.astype(F32),axis=0,keepdims=True))
    out=m2+dg(act_s[rows,:],wd_ref[...],1,0)+bd_ref[...]
    out_ref[...]=out.astype(BF).reshape(FA,SB,D)
    dn3=dg(gp_s[rows,:],wu_ref[...],1,1)
    dg3=jnp.sum(dn3*xh3,axis=0,keepdims=True)
    db3=jnp.sum(dn3,axis=0,keepdims=True)
    cotf=cot.astype(F32)
    gm2=cotf+ln_back(dn3,xh3,r3,g3_ref[...])
    rr=gm2.astype(BF)
    r_s[rows,:]=rr
    dot=dg(wo_ref[...],rr,1,1)
    for p in range(D//128):
        vp=jnp.concatenate([v_s[:,p*128:p*128+128],vb],axis=1)
        kt=k_s[:,p*128:p*128+128].T
        for u in range(2):
            h=2*p+u
            hs=slice(h*64,h*64+64)
            rl=rls[h]
            do=dot[hs,:]
            dd=jnp.sum(do*ht_s[hs,cols].astype(F32),axis=0,keepdims=True)*rl
            dob=(do*rl).astype(BF)
            d3=[-z.astype(F32) for z in split3(dd)]
            dp=dg(vp,pad_head(dob,u,row_block(d3,R)),1,0)
            e=e_s[h]
            ds=(e.astype(F32)*dp).astype(BF)
            dpt_s[2*D+h*64:2*D+h*64+64,cols]=dg(dob,e,1,1).astype(BF)
            dpt_s[D+h*64:D+h*64+64,cols]=(dg(qt_s[hs,:],ds,1,1)*LN2).astype(BF)
            dpt_s[h*64:h*64+64,cols]=(dg(kt[u*64:u*64+64],ds,1,0)*0.125).astype(BF)
    dn2=dg(dpt_s[:,cols],w_ref[...],0,1).astype(BF).astype(F32)
    dg2=jnp.sum(dn2*xh2,axis=0,keepdims=True)
    db2=jnp.sum(dn2,axis=0,keepdims=True)
    gm_ref[...]=(gm2+ln_back(dn2,xh2,r2,g2_ref[...])).astype(BF).reshape(FA,SB,D)
    small=[dg2,db2,dg3,db3,jnp.sum(cotf,axis=0,keepdims=True)]
    @pl.when(i==0)
    def _():
        dv_ref[...]=jnp.zeros_like(dv_ref)
        dbu_ref[...]=jnp.zeros_like(dbu_ref)
    for j,z in enumerate(small):
        dv_ref[j:j+1]+=z
    for q,z in enumerate(dbu):
        dbu_ref[0:1,q*C:q*C+C]+=z
    @pl.when(i==last)
    def _():
        dwo_ref[...]=dg(ht_s[...],r_s[...],1,0).astype(BF)
        for q in range(3):
            dw_ref[:,q*D:q*D+D]=dg(n2_s[...],dpt_s[q*D:q*D+D,:],0,1).astype(BF)
        for q in range(wu_ref.shape[1]//C):
            cs=slice(q*C,q*C+C)
            dwu_ref[:,cs]=dg(n3_s[...],gp_s[:,cs],0,0).astype(BF)
            dwd_ref[cs,:]=dg(act_s[:,cs],cot_s[...],0,0).astype(BF)

def run_b(t, cnt, m, cot, g2,b2,w,wo,g3,b3,wu,bu,wd,bd, SB=16):
    FA,SL,D=m.shape; FF=wu.shape[1]; R=FA*SB; N=FA*SL
    row=pl.BlockSpec((FA,SB,D),lambda i,s:(0,i,0))
    one=lambda *sh: pl.BlockSpec(sh,lambda i,s:(0,)*len(sh),pipeline_mode=pl.Buffered(1))
    con=lambda *sh: pl.BlockSpec(sh,lambda i,s:(0,)*len(sh))
    gs=pltpu.PrefetchScalarGridSpec(num_scalar_prefetch=1,grid=(SL//SB,),
        in_specs=[row,row,one(1,D),one(1,D),one(D,3*D),one(D,D),one(1,D),one(1,D),one(D,FF),one(1,FF),one(FF,D),one(1,D)],
        out_specs=[row,row,con(D,3*D),con(D,D),con(D,FF),con(FF,D),con(8,D),con(8,FF)],
        scratch_shapes=[pltpu.VMEM((N,D),BF),pltpu.VMEM((N,D),BF),pltpu.VMEM((N,D),BF),pltpu.VMEM((D,N),BF),pltpu.VMEM((3*D,N),BF),
            pltpu.VMEM((N,FF),BF),pltpu.VMEM((N,FF),BF),pltpu.VMEM((N,D),BF),
            pltpu.VMEM((D,R),BF),pltpu.VMEM((R,D),BF),pltpu.VMEM((R,D),BF),pltpu.VMEM((D//64,R,R),BF),pltpu.VMEM((8,128),F32)])
    sd=jax.ShapeDtypeStruct
    r=lambda z:z.reshape(1,-1)
    return pl.pallas_call(partial(b_kernel,t,SB),grid_spec=gs,
        out_shape=[sd((FA,SL,D),BF),sd((FA,SL,D),BF),sd((D,3*D),BF),sd((D,D),BF),sd((D,FF),BF),sd((FF,D),BF),sd((8,D),F32),sd((8,FF),F32)],
        compiler_params=pltpu.CompilerParams(vmem_limit_bytes=60<<20),name="middle",
        cost_estimate=pl.CostEstimate(flops=50_000_000_000,bytes_accessed=20<<20,transcendentals=4<<20))(cnt,m,cot,r(g2),r(b2),w,wo,r(g3),r(b3),wu,r(bu),wd,r(bd))

from jax.sharding import PartitionSpec as P


def gather_sum(pieces):
    total=pieces[0].astype(F32)
    for z in pieces[1:]:
        total=total+z.astype(F32)
    return total

def pick(a,i,axis=0):
    return lax.dynamic_index_in_dim(a,i,axis,keepdims=False)

def reduce_rows(g):
    nf,rw,D=g.shape
    nt=lax.axis_size("task")
    f=lax.axis_index("feat"); t=lax.axis_index("task")
    c=f%2; z=f//2; nz=nf//2
    gp=g.reshape(nz,2,rw,D)
    got=lax.ppermute(pick(gp,1-c,1),"feat",[(i,i^1) for i in range(nf)])
    s=gather_sum([pick(gp,c,1),got]).astype(BF).reshape(nz,nt,rw//nt,D)
    s=gather_sum([pick(s,t,1)]+[lax.ppermute(pick(s,t^r,1),"task",[(i,i^r) for i in range(nt)]) for r in range(1,nt)]).astype(BF)
    s=gather_sum([pick(s,z)]+[lax.ppermute(pick(s,z^r),"feat",[(i,i^(2*r)) for i in range(nf)]) for r in range(1,nz)]).astype(BF)
    every=jnp.stack([s]+[lax.ppermute(s,"task",[(i,i^r) for i in range(nt)]) for r in range(1,nt)])
    every=jnp.concatenate([pick(every,t^i)[None] for i in range(nt)])
    return every.reshape(rw,D).astype(F32)

def middle_plain(t,cnt,m,cot,g2,b2,w,wo,g3,b3,wu,bu,wd,bd):
    FA=m.shape[0]; D=m.shape[-1]; H=D//64
    mf=m.astype(F32)
    def norm(v,g,b):
        c,r=ln_stats(v)
        return c*r*g+b
    mm=lambda a,b: jnp.einsum("fsd,de->fse",a,b,preferred_element_type=F32)
    mt=lambda a,b: jnp.einsum("fse,de->fsd",a,b,preferred_element_type=F32)
    out_sum=lambda a,b: jnp.einsum("fsd,fse->de",a,b,preferred_element_type=F32).astype(BF)
    n2=norm(mf,g2,b2).astype(BF)
    q,k,v=[z[...,0,:,:] for z in jnp.split(mm(n2,w).astype(BF).reshape(m.shape[:2]+(3,H,64)),3,axis=2)]
    keep=jnp.arange(FA)<cnt[t]
    s=jnp.where(keep,jnp.einsum("qshe,kshe->shqk",q,k,preferred_element_type=F32)*0.125,-1e30)
    pr=jax.nn.softmax(s,axis=-1)
    h2=jnp.einsum("shqk,kshe->qshe",pr.astype(BF),v,preferred_element_type=F32).astype(BF).reshape(m.shape)
    m2=mf+mm(h2,wo)
    n3,back3=jax.vjp(norm,m2,g3,b3)
    n3=n3.astype(BF)
    pre=mm(n3,wu)+bu
    act,back=jax.vjp(partial(jax.nn.gelu,approximate=False),pre)
    act=act.astype(BF)
    out=(m2+mm(act,wd)+bd).astype(BF)
    gp=back(mt(cot,wd))[0].astype(BF)
    a,dg3,db3=back3(mt(gp,wu))
    gm2=cot.astype(F32)+a
    rr=gm2.astype(BF)
    do=mt(rr,wo).astype(BF).reshape(q.shape)
    dp=jnp.einsum("qshe,kshe->shqk",do,v,preferred_element_type=F32)
    ds=(pr*(dp-jnp.sum(pr*dp,axis=-1,keepdims=True))).astype(BF)
    dq=jnp.einsum("shqk,kshe->qshe",ds,k,preferred_element_type=F32)*0.125
    dk=jnp.einsum("shqk,qshe->kshe",ds,q,preferred_element_type=F32)*0.125
    dv=jnp.einsum("shqk,qshe->kshe",pr.astype(BF),do,preferred_element_type=F32)
    dpk=jnp.stack([dq,dk,dv],axis=2).reshape(m.shape[:2]+(3*D,)).astype(BF)
    _,back2=jax.vjp(norm,mf,g2,b2)
    a,dg2,db2=back2(mt(dpk,w).astype(BF).astype(F32))
    small=jnp.concatenate([jnp.stack([dg2,db2,dg3,db3,jnp.sum(cot.astype(F32),axis=(0,1))]),jnp.zeros((3,D),F32)])
    dbu=jnp.sum(gp.astype(F32),axis=(0,1))[None]
    return out,(gm2+a).astype(BF),out_sum(n2,dpk),out_sum(h2,rr),out_sum(n3,gp),out_sum(act,cot),small,dbu

def move(a):
    return lax.all_to_all(a,"feat",0,0)

def body(x,cot,lens,cnt,g1,b1,w1,wo1,g2,b2,w2,wo2,g3,b3,wu,bu,wd,bd):
    T,F,S,D=x.shape
    FF=wu.shape[1]
    nf=lax.axis_size("feat")
    sl=S//nf; FA=F*nf
    chunk=lambda a: a.reshape(nf,F,sl,D)
    spread=lambda a: a.reshape(F,nf,sl,D).swapaxes(0,1)
    rejoin=lambda a: a.swapaxes(0,1).reshape(F,S,D)
    cots=[move(spread(cot[t])) for t in range(T)]
    saved=[]; mids=[]
    for t in range(T):
        o=run_a(t,lens,x,g1,b1,w1,wo1,nf)
        mids.append(move(o[0])); saved.append(o[1:])
    mid_fn=run_b if FA*16<=256 else middle_plain
    outs=[]; gms=[]; mg=[]
    for t in range(T):
        o=mid_fn(t,cnt,mids[t].reshape(FA,sl,D),cots[t].reshape(FA,sl,D),g2,b2,w2,wo2,g3,b3,wu,bu,wd,bd)
        gms.append(move(chunk(o[1])))
        outs.append(move(chunk(o[0])))
        mg.append(o[2:])
    add=lambda i: gather_sum([m[i] for m in mg])
    rp=D//nf; fp=FF//nf
    blocks=lambda a: a.reshape(nf,rp,a.shape[1]//D,D).swapaxes(1,2).reshape(nf,-1,D)
    def with_vectors(mats,vecs):
        v=jnp.concatenate([z.reshape(-1,D) for z in vecs])
        v=jnp.pad(v,((0,32-v.shape[0]),(0,0)))
        return jnp.concatenate([z.astype(BF) for z in mats]+[jnp.broadcast_to(v.astype(BF)[None],(nf,)+v.shape)],axis=1)
    gmid=with_vectors([blocks(add(0)),blocks(add(1)),blocks(add(2)),add(3).reshape(nf,fp,D)],[add(4)[:5],add(5)[:1]])
    rmid=reduce_rows(gmid)
    dxs=[]; cg=[]
    for t in range(T):
        o=run_c(t,lens,x,gms[t],g1,b1,w1,wo1,*saved[t])
        dxs.append(o[0]); cg.append(o[1:])
    addc=lambda i: gather_sum([m[i] for m in cg])
    rlate=reduce_rows(with_vectors([blocks(addc(0)),blocks(addc(1))],[addc(2)[:2]]))
    f=lax.axis_index("feat")
    unblock=lambda a: a.reshape(-1,rp,D).swapaxes(0,1).reshape(rp,-1)
    vec=lambda a,i: lax.dynamic_slice_in_dim(a[i],f*rp,rp)
    ml=4*rp
    mm=8*rp+fp
    mv=rmid[mm:]; lv=rlate[ml:]
    dbu=lax.dynamic_slice_in_dim(mv[5:5+FF//D].reshape(FF),f*fp,fp)
    return (jnp.stack([rejoin(o) for o in outs]), jnp.stack(dxs),
        vec(lv,0),vec(lv,1),unblock(rlate[:3*rp]),unblock(rlate[3*rp:4*rp]),
        vec(mv,0),vec(mv,1),unblock(rmid[:3*rp]),unblock(rmid[3*rp:4*rp]),
        vec(mv,2),vec(mv,3),unblock(rmid[4*rp:8*rp]),dbu,rmid[8*rp:8*rp+fp],vec(mv,4))

def solution(mesh):
    rows=P("task","feat",None,None)
    mat=P("feat",None)
    return jax.shard_map(body,mesh=mesh,
        in_specs=(rows,rows,P("task"),P("task"))+(P(),)*14,
        out_specs=(rows,rows,P("feat"),P("feat"),mat,mat,P("feat"),P("feat"),mat,mat,P("feat"),P("feat"),mat,P("feat"),mat,P("feat")),
        check_vma=False)
```

```python
import math
from functools import partial
import jax, jax.numpy as jnp
from jax import lax
from jax.experimental import pallas as pl
from jax.experimental.pallas import tpu as pltpu
BF=jnp.bfloat16; F32=jnp.float32
EPS=1e-5
LOG2E=1.4426950408889634
QS=0.125*LOG2E

def dg(a,b,ca,cb):
    return lax.dot_general(a,b,(((ca,),(cb,)),((),())),preferred_element_type=F32)

def ln_stats(v):
    mean=jnp.mean(v,axis=-1,keepdims=True)
    c=v-mean
    var=jnp.mean(c*c,axis=-1,keepdims=True)
    return c, lax.rsqrt(var+EPS)

def split3(v):
    a=v.astype(BF); r=v-a.astype(F32)
    b=r.astype(BF); r=r-b.astype(F32)
    return a,b,r.astype(BF)

def pad_head(rows,u,aug):
    z=jnp.zeros_like(rows)
    return jnp.concatenate([rows,z,aug] if u==0 else [z,rows,aug],axis=0)

def lane_block(cols,n):
    lane=lax.broadcasted_iota(jnp.int32,(n,128),1)
    out=jnp.zeros((n,128),F32)
    for i,c in enumerate(cols):
        out=jnp.where(lane==i,c,out)
    return out.astype(BF)

def row_block(rows,n):
    sub=lax.broadcasted_iota(jnp.int32,(128,n),0)
    out=jnp.zeros((128,n),F32)
    for i,r in enumerate(rows):
        out=jnp.where(sub==i,r,out)
    return out.astype(BF)

def staged(n,ahead,first,second,third):
    got=[first(i) for i in range(min(ahead,n))]
    last=None
    for i in range(n):
        if i+ahead<n:
            got.append(first(i+ahead))
        if last is not None:
            third(*last)
        last=(i,*second(i,got[i]))
        got[i]=None
    third(*last)

def a_kernel(t, both, len_ref, x_ref, *refs):
    if both:
        cot_ref,refs=refs[0],refs[1:]
    g_ref, b_ref, w_ref, wo_ref, *mid_refs, qt_ref, k_ref, v_ref, ht_ref, l_ref, mid_s=refs
    S,D=x_ref.shape[2:]
    x=x_ref[0,0].astype(F32)
    c,r=ln_stats(x)
    n1=(c*r*g_ref[...]+b_ref[...]).astype(BF)
    qt_ref[0]=(dg(w_ref[:,0:D],n1,0,1)*QS).astype(BF)
    k_ref[0]=dg(n1,w_ref[:,D:2*D],1,0).astype(BF)
    v_ref[0]=dg(n1,w_ref[:,2*D:3*D],1,0).astype(BF)
    n=len_ref[t]
    ks=lax.broadcasted_iota(jnp.int32,(S,1),0)
    bias=jnp.where(ks<n,0.0,-1e30)
    kb=lane_block([bias],S)
    qa=row_block([jnp.ones((1,S),F32)],S)
    ones=jnp.ones((16,S),BF)
    H=D//64; C=256
    units=[(h,c) for h in range(H) for c in range(0,S,C)]
    def scores(n):
        h,c=units[n]; p=h//2
        kp=jnp.concatenate([k_ref[0,:,p*128:p*128+128],kb],axis=1)
        return dg(kp,pad_head(qt_ref[0,h*64:h*64+64,c:c+C],h%2,qa[:,c:c+C]),1,0)
    vts={}
    def finish(n,e,m):
        h,c=units[n]
        if h//2 not in vts:
            vts[h//2]=v_ref[0,:,h//2*128:h//2*128+128].T
        va=jnp.concatenate([vts[h//2][h%2*64:h%2*64+64],ones],axis=0)
        o=dg(va,e,1,0)
        l=o[64:65]
        ht_ref[0,h*64:h*64+64,c:c+C]=(o[:64]*(1.0/l)).astype(BF)
        l_ref[0,h:h+1,c:c+C]=m+jnp.log2(l)
    def weigh(n,s):
        m=jnp.max(s,axis=0,keepdims=True)
        return jnp.exp2(s-m).astype(BF),m
    staged(len(units),2,scores,weigh,finish)
    mid_s[...]=x+dg(ht_ref[0],wo_ref[...],0,0)
    if len(mid_refs)==1:
        mid_ref=mid_refs[0]; nd=mid_ref.shape[0]; sl=S//nd
        for j in range(nd):
            mid_ref[j,0,0]=mid_s[j*sl:(j+1)*sl].astype(BF)
            if both:
                mid_ref[j,1,0]=cot_ref[0,0,j*sl:(j+1)*sl,:]
    else:
        nd=len(mid_refs); sl=S//nd; me=len_ref[len_ref.shape[0]-1]
        for r in range(nd):
            mid_refs[r][0]=mid_s[pl.ds(pl.multiple_of((r^me)*sl,sl),sl)].astype(BF)

def run_a(t, lens, x, cot, g, b, w, wo, nd, pieces):
    T,F,S,D=x.shape
    both=cot is not None
    kinds=2 if both else 1
    row=pl.BlockSpec((1,1,S,D),lambda f,s:(t,f,0,0))
    one=lambda *sh: pl.BlockSpec(sh,lambda f,s:(0,)*len(sh),pipeline_mode=pl.Buffered(1))
    per=lambda *sh: pl.BlockSpec((1,)+sh,lambda f,s:(f,0,0))
    sd=jax.ShapeDtypeStruct
    if pieces:
        out_specs=[per(S//nd,D)]*nd; out_shape=[sd((F,S//nd,D),BF)]*nd
    else:
        out_specs=[pl.BlockSpec((nd,kinds,1,S//nd,D),lambda f,s:(0,0,f,0,0))]; out_shape=[sd((nd,kinds,F,S//nd,D),BF)]
    n=len(out_specs)
    gs=pltpu.PrefetchScalarGridSpec(num_scalar_prefetch=1,grid=(F,),
        in_specs=[row]*kinds+[one(1,D),one(1,D),one(D,3*D),one(D,D)],
        out_specs=out_specs+[per(D,S),per(S,D),per(S,D),per(D,S),per(D//64,S)],scratch_shapes=[pltpu.VMEM((S,D),F32)])
    o=pl.pallas_call(partial(a_kernel,t,both),grid_spec=gs,
        out_shape=out_shape+[sd((F,D,S),BF),sd((F,S,D),BF),sd((F,S,D),BF),sd((F,D,S),BF),sd((F,D//64,S),F32)],
        compiler_params=pltpu.CompilerParams(vmem_limit_bytes=60<<20),name="fwd_samples",
        cost_estimate=pl.CostEstimate(flops=2_000_000_000,bytes_accessed=1<<20,transcendentals=0))(
            lens,*([x,cot] if both else [x]),g.reshape(1,D),b.reshape(1,D),w,wo)
    return (o[:n] if pieces else o[0]),o[n:]

LN2=0.6931471805599453

def ln_back(dn,xh,r,gain):
    gd=dn*gain
    return r*(gd-jnp.mean(gd,axis=-1,keepdims=True)-xh*jnp.mean(gd*xh,axis=-1,keepdims=True))

def put(mine_ref,oth_ref,core,at,acc,prev_ref):
    half=mine_ref.shape[0]; rp=acc.shape[0]//(2*half)
    if isinstance(at,int):
        at=pl.ds(at,rp)
    for j in range(half):
        even=acc[2*j*rp:(2*j+1)*rp]; odd=acc[(2*j+1)*rp:(2*j+2)*rp]
        if prev_ref is not None:
            even=even+prev_ref[2*j,at].astype(F32); odd=odd+prev_ref[2*j+1,at].astype(F32)
        mine_ref[j,at]=jnp.where(core==0,even,odd).astype(BF)
        oth_ref[j,at]=jnp.where(core==0,odd,even).astype(BF)

def put_all(g_ref,at,acc):
    n=g_ref.shape[0]; rp=acc.shape[0]//n
    if isinstance(at,int):
        at=pl.ds(at,rp)
    for j in range(n):
        g_ref[j,at]=acc[j*rp:(j+1)*rp].astype(BF)

def c_kernel(t, len_ref, x_ref, gm_ref, g_ref, b_ref, wo_ref, qt_ref, k_ref, v_ref, ht_ref, l_ref, *refs):
    S,D=x_ref.shape[2:]
    if t==0:
        dpt_ref, gr_ref, dot_ref, acc_ref=refs
    else:
        prev_ref, dpt_ref, mine_ref, oth_ref, dot_ref, acc_ref=refs
    f=pl.program_id(0); last=pl.num_programs(0)-1
    c,r=ln_stats(x_ref[0,0].astype(F32))
    n1=(c*r*g_ref[...]+b_ref[...]).astype(BF)
    nd=gm_ref.shape[0]
    s_in=jnp.concatenate([gm_ref[j,0,0] for j in range(nd)],axis=0)
    dot_ref[...]=dg(wo_ref[...],s_in,1,1).astype(BF)
    n=len_ref[t]
    ks=lax.broadcasted_iota(jnp.int32,(S,1),0)
    bias=jnp.where(ks<n,0.0,-1e30)
    one=jnp.ones((S,1),F32)
    kb=lane_block([bias,one,one,one],S)
    vb=lane_block([one,one,one],S)
    oner=jnp.ones((1,S),F32)
    C=256
    units=[(h,c) for h in range(D//64) for c in range(0,S,C)]
    kts={}
    def first(n):
        h,c=units[n]; p=h//2
        kp=jnp.concatenate([k_ref[0,:,p*128:p*128+128],kb],axis=1)
        vp=jnp.concatenate([v_ref[0,:,p*128:p*128+128],vb],axis=1)
        hs=slice(h*64,h*64+64)
        do=dot_ref[hs,c:c+C]
        dd=jnp.sum(do.astype(F32)*ht_ref[0,hs,c:c+C].astype(F32),axis=0,keepdims=True)
        l3=[-z.astype(F32) for z in split3(l_ref[0,h:h+1,c:c+C])]
        d3=[-z.astype(F32) for z in split3(dd)]
        s=dg(kp,pad_head(qt_ref[0,hs,c:c+C],h%2,row_block([oner[:,:C]]+l3,C)),1,0)
        return s,dg(vp,pad_head(do,h%2,row_block(d3,C)),1,0)
    def second(n,sd):
        e=jnp.exp2(sd[0])
        return e.astype(BF),(e*sd[1]).astype(BF)
    def third(n,e,ds):
        h,c=units[n]
        hs=slice(h*64,h*64+64)
        if h//2 not in kts:
            kts[h//2]=k_ref[0,:,h//2*128:h//2*128+128].T
        dv=dg(dot_ref[hs,c:c+C],e,1,1)
        dk=dg(qt_ref[0,hs,c:c+C],ds,1,1)*LN2
        if C<S:
            if c==0:
                part[h]=(dv,dk)
            else:
                dv=dv+part[h][0]; dk=dk+part[h][1]
                if c+C<S: part[h]=(dv,dk)
        if c+C==S:
            dpt_ref[0,2*D+h*64:2*D+h*64+64,:]=dv.astype(BF)
            dpt_ref[0,D+h*64:D+h*64+64,:]=dk.astype(BF)
        dpt_ref[0,h*64:h*64+64,c:c+C]=(dg(kts[h//2][h%2*64:h%2*64+64],ds,1,0)*0.125).astype(BF)
    part={}
    staged(len(units),1,first,second,third)
    grads=lambda i: dg(ht_ref[0],s_in,1,0) if i==3 else dg(n1,dpt_ref[0,i*D:i*D+D,:],0,1)
    @pl.when(f==0)
    def _():
        for i in range(4):
            acc_ref[i]=grads(i)
    @pl.when((f>0)&(f<last))
    def _():
        for i in range(4):
            acc_ref[i]+=grads(i)
    @pl.when(f==last)
    def _():
        rp=D//nd
        for i in range(4):
            if t==0:
                put_all(gr_ref,i*rp,acc_ref[i]+grads(i))
            else:
                put(mine_ref,oth_ref,len_ref[len_ref.shape[0]-1]%2,i*rp,acc_ref[i]+grads(i),prev_ref)

def run_c(t, lens, x, gm, g, b, wo, qt, k, v, ht, l, prev=None):
    T,F,S,D=x.shape; nd=gm.shape[0]; rw=4*(D//nd)
    one=lambda *sh: pl.BlockSpec(sh,lambda f,s:(0,)*len(sh),pipeline_mode=pl.Buffered(1))
    con=lambda *sh: pl.BlockSpec(sh,lambda f,s:(0,)*len(sh))
    per=lambda *sh: pl.BlockSpec((1,)+sh,lambda f,s:(f,0,0))
    in_specs=[pl.BlockSpec((1,1,S,D),lambda f,s:(t,f,0,0)),
              pl.BlockSpec((nd,1,1,S//nd,D),lambda f,s:(0,0,f,0,0)),
              one(1,D),one(1,D),one(D,D),per(D,S),per(S,D),per(S,D),per(D,S),per(D//64,S)]
    args=[lens,x,gm,g.reshape(1,D),b.reshape(1,D),wo,qt,k,v,ht,l]
    sd=jax.ShapeDtypeStruct
    out_specs=[per(3*D,S)]
    out_shape=[sd((F,3*D,S),BF)]
    if t==0:
        out_specs.append(con(nd,rw,D)); out_shape.append(sd((nd,rw,D),BF))
    else:
        out_specs+=[con(nd//2,rw,D)]*2; out_shape+=[sd((nd//2,rw,D),BF)]*2
        in_specs.append(one(nd,rw,D)); args.append(prev)
    gs=pltpu.PrefetchScalarGridSpec(num_scalar_prefetch=1,grid=(F,),in_specs=in_specs,out_specs=out_specs,
        scratch_shapes=[pltpu.VMEM((D,S),BF),pltpu.VMEM((4,D,D),F32)])
    return pl.pallas_call(partial(c_kernel,t),grid_spec=gs,out_shape=out_shape,
        compiler_params=pltpu.CompilerParams(vmem_limit_bytes=60<<20),name="bwd_samples",
        cost_estimate=pl.CostEstimate(flops=2_000_000_000,bytes_accessed=1<<20,transcendentals=0))(*args)

def e_kernel(nout, x_ref, gm_ref, dpt_ref, g_ref, w_ref, *refs):
    outs,refs=refs[:nout],refs[nout:]
    dx_ref,vec_ref=refs[-2-(nout>0)],refs[-1]
    x=x_ref[0,0].astype(F32)
    c,r=ln_stats(x)
    xh=c*r
    nd=gm_ref.shape[0]; sl=gm_ref.shape[3]
    s_in=jnp.concatenate([gm_ref[j,0,0] for j in range(nd)],axis=0).astype(F32)
    dn=dg(dpt_ref[0],w_ref[...],0,1)
    @pl.when(pl.program_id(0)==0)
    def _():
        vec_ref[...]=jnp.zeros_like(vec_ref)
    vec_ref[0:1]+=jnp.sum(dn*xh,axis=0,keepdims=True)
    vec_ref[1:2]+=jnp.sum(dn,axis=0,keepdims=True)
    dx_ref[0,0]=(s_in+ln_back(dn,xh,r,g_ref[...])).astype(BF)
    if nout:
        for t in range(nout):
            for j in range(nd):
                refs[-2][t,0,j*sl:(j+1)*sl,:]=outs[t][j,0,0]

def run_e(t, x, gm, dpt, g, w, dx=None, outs=()):
    T,F,S,D=x.shape; nd=gm.shape[0]; nout=len(outs)
    one=lambda *sh: pl.BlockSpec(sh,lambda f:(0,)*len(sh),pipeline_mode=pl.Buffered(1))
    piece=lambda k: pl.BlockSpec((nd,1,1,S//nd,D),lambda f:(0,k,f,0,0))
    in_specs=[pl.BlockSpec((1,1,S,D),lambda f:(t,f,0,0)),piece(0),pl.BlockSpec((1,3*D,S),lambda f:(f,0,0)),one(1,D),one(D,3*D)]
    in_specs+=[piece(o.shape[1]-1) for o in outs]
    args=[x,gm,dpt,g.reshape(1,D),w,*outs]
    sd=jax.ShapeDtypeStruct
    out_specs=[pl.BlockSpec((1,1,S,D),lambda f:(t,f,0,0))]
    out_shape=[sd((T,F,S,D),BF)]
    if nout:
        out_specs.append(pl.BlockSpec((T,1,S,D),lambda f:(0,f,0,0))); out_shape.append(sd((T,F,S,D),BF))
    out_specs.append(pl.BlockSpec((8,D),lambda f:(0,0))); out_shape.append(sd((8,D),F32))
    alias={}
    if dx is not None:
        in_specs.append(pl.BlockSpec(memory_space=pl.ANY)); args.append(dx)
        alias={len(args)-1:0}
    return pl.pallas_call(partial(e_kernel,nout),grid=(F,),in_specs=in_specs,out_specs=out_specs,out_shape=out_shape,input_output_aliases=alias,
        compiler_params=pltpu.CompilerParams(vmem_limit_bytes=60<<20),name="input_grads",
        cost_estimate=pl.CostEstimate(flops=1_000_000_000,bytes_accessed=1<<20,transcendentals=0))(*args)

def out_kernel(nt, *refs):
    ins,out_ref=refs[:nt],refs[nt]
    for t in range(nt):
        nd=ins[t].shape[0]; sl=ins[t].shape[3]
        for j in range(nd):
            out_ref[t,0,j*sl:(j+1)*sl,:]=ins[t][j,0,0]

def run_out(outs):
    nd,_,F,sl,D=outs[0].shape; T=len(outs)
    return pl.pallas_call(partial(out_kernel,T),grid=(F,),
        in_specs=[pl.BlockSpec((nd,1,1,sl,D),lambda f,k=o.shape[1]-1:(0,k,f,0,0)) for o in outs],
        out_specs=pl.BlockSpec((T,1,nd*sl,D),lambda f:(0,f,0,0)),out_shape=jax.ShapeDtypeStruct((T,F,nd*sl,D),BF),
        compiler_params=pltpu.CompilerParams(vmem_limit_bytes=40<<20),name="rows_in_order",
        cost_estimate=pl.CostEstimate(flops=0,bytes_accessed=1<<20,transcendentals=0))(*outs)

def finish_kernel(km, kl, rp, fp, t_ref, *refs):
    nt=(len(refs)-8)//2
    mids,lates=refs[:nt],refs[nt:2*nt]
    up_ref,down_ref,qkv2_ref,out2_ref,qkv1_ref,out1_ref,mid_s,late_s=refs[2*nt:]
    t=t_ref[0]; D=mid_s.shape[1]; nq=up_ref.shape[1]//D
    for r in range(nt):
        mid_s[pl.ds(pl.multiple_of((r^t)*km,8),km)]=mids[r][...].astype(F32)
        late_s[pl.ds(pl.multiple_of((r^t)*kl,8),kl)]=lates[r][0:kl].astype(F32)
    for q in range(nq):
        up_ref[:,q*D:q*D+D]=mid_s[q*rp:q*rp+rp]
    b=nq*rp
    down_ref[...]=mid_s[b:b+fp]
    b+=fp
    for q in range(3):
        qkv2_ref[:,q*D:q*D+D]=mid_s[b+q*rp:b+q*rp+rp]
        qkv1_ref[:,q*D:q*D+D]=late_s[q*rp:q*rp+rp]
    out2_ref[...]=mid_s[b+3*rp:b+4*rp]
    out1_ref[...]=late_s[3*rp:4*rp]

def run_finish(t, mids, lates, km, kl, rp, fp, FF):
    nt=len(mids); D=mids[0].shape[1]
    v=pl.BlockSpec(memory_space=pltpu.VMEM)
    sd=lambda *s: jax.ShapeDtypeStruct(s,F32)
    return pl.pallas_call(partial(finish_kernel,km,kl,rp,fp),in_specs=[pl.BlockSpec(memory_space=pltpu.SMEM)]+[v]*(2*nt),out_specs=[v]*6,
        out_shape=[sd(rp,FF),sd(fp,D),sd(rp,3*D),sd(rp,D),sd(rp,3*D),sd(rp,D)],
        scratch_shapes=[pltpu.VMEM((nt*km,D),F32),pltpu.VMEM((nt*kl,D),F32)],
        compiler_params=pltpu.CompilerParams(vmem_limit_bytes=40<<20),name="grads_in_order",
        cost_estimate=pl.CostEstimate(flops=0,bytes_accessed=1<<20,transcendentals=0))(t,*mids,*lates)


def phi_pair(v):
    a=jnp.abs(v)
    t=1.0/(1.0+(0.3275911*0.7071067811865476)*a)
    e=jnp.exp2(v*v*(-0.5*LOG2E))
    y=t*(0.5*0.254829592+t*(0.5*-0.284496736+t*(0.5*1.421413741+t*(0.5*-1.453152027+t*(0.5*1.061405429)))))
    y=y*e
    return jnp.where(v<0,y,1.0-y), e*0.3989422804014327

def loop(n,rolled):
    def run(f):
        if rolled and n>1:
            pl.loop(0,n)(f)
        else:
            for i in range(n):
                f(i)
    return run

def mult(v,n):
    return v if isinstance(v,int) else pl.multiple_of(v,n)

def b_kernel(t, SB, nm, cnt_ref, *refs):
    m_refs,refs=refs[:nm],refs[nm:]
    cot_ref, g2_ref, b2_ref, w_ref, wo_ref, g3_ref, b3_ref, wu_ref, bu_ref, wd_ref, bd_ref, *refs=refs
    nd,_,F,_,D=cot_ref.shape
    FA=nd*F; H=D//64; FF=wu_ref.shape[1]
    if t==0:
        rows_ref,gr_ref,vec_s,*refs=refs
    else:
        prev_hbm,gm_ref,out_ref,mine_ref,oth_ref,vec_s,*refs=refs
        prev_ref,sem=refs[-2:]; refs=refs[:-2]
    n2_s, n3_s, r_s, ht_s, dpt_s, act_s, gp_s, cot_s, qt_s, k_s, v_s, e_s, m_s, rl_s, dot_s=refs
    G=FA*16; NG=SB//16; R=G*NG
    i=pl.program_id(0); last=pl.num_programs(0)-1
    if t>0:
        prev=pltpu.make_async_copy(prev_hbm,prev_ref,sem)
        @pl.when(i==0)
        def _():
            prev.start()
    at=pl.multiple_of(i*R,R); rows=pl.ds(at,R)
    split=lambda v: jnp.concatenate([v[:,g*16:g*16+16].reshape(-1,D) for g in range(NG)],axis=0)
    def join(v,ref,kind):
        for g in range(NG):
            ref[:,kind,:,g*16:g*16+16,:]=v[g*G:g*G+G].reshape(nd,F,16,D)
    if nm==1:
        m=split(m_refs[0][...].reshape(FA,SB,D).astype(F32))
    else:
        me=cnt_ref[cnt_ref.shape[0]-1]
        for r in range(nm):
            for g in range(NG):
                m_s[pl.ds(pl.multiple_of((r^me)*(F*16)+g*G,F*16),F*16)]=m_refs[r][:,g*16:g*16+16].reshape(F*16,D).astype(F32)
        m=m_s[...]
    c,r2=ln_stats(m)
    xh2=c*r2
    n2=(xh2*g2_ref[...]+b2_ref[...]).astype(BF)
    n2_s[rows,:]=n2
    qt_s[...]=(dg(w_ref[:,0:D],n2,0,1)*QS).astype(BF)
    k_s[...]=dg(n2,w_ref[:,D:2*D],1,0).astype(BF)
    v_s[...]=dg(n2,w_ref[:,2*D:3*D],1,0).astype(BF)
    n=cnt_ref[t]
    krow=lax.broadcasted_iota(jnp.int32,(G,128),0)
    lane=lax.broadcasted_iota(jnp.int32,(G,128),1)
    kb=jnp.where(lane==0,jnp.where(krow//16>=n,-1e30,0.0),jnp.where(lane-1==krow%16,-1e30,0.0)).astype(BF)
    vb=jnp.where(lane<3,1.0,0.0).astype(BF)
    qcol=lax.broadcasted_iota(jnp.int32,(128,G),1)
    sub=lax.broadcasted_iota(jnp.int32,(128,G),0)
    qa=jnp.where((sub==0)|((sub<=16)&(sub-1!=qcol%16)),1.0,0.0).astype(BF)
    ones=jnp.ones((16,G),BF)
    pair=lambda h: slice(h//2*128,h//2*128+128)
    head=lambda h: slice(h*64,h*64+64)
    def flipper(ref,gs):
        flips={}
        def flip(h):
            if h//2 not in flips:
                flips[h//2]=ref[gs,pair(h)].T
            return flips[h//2][h%2*64:h%2*64+64]
        return flip
    def group(g):
        return pl.ds(mult(g*G,G),G),pl.ds(pl.multiple_of(at+g*G,G),G)
    @loop(NG,False)
    def _(g):
        gs,ps=group(g)
        flip=flipper(v_s,gs)
        def first(h):
            return dg(jnp.concatenate([k_s[gs,pair(h)],kb],axis=1),pad_head(qt_s[head(h),gs],h%2,qa),1,0)
        def second(h,s):
            e=jnp.exp2(s-jnp.max(s,axis=0,keepdims=True)).astype(BF)
            e_s[g*H+h]=e
            return (e,)
        def third(h,e):
            o=dg(jnp.concatenate([flip(h),ones],axis=0),e,1,0)
            rl=1.0/o[64:65]
            rl_s[g,h:h+1]=rl
            ht_s[head(h),ps]=(o[:64]*rl).astype(BF)
        staged(H,2,first,second,third)
    @pl.when(i==0)
    def _():
        vec_s[...]=jnp.zeros_like(vec_s)
    m2=m+dg(ht_s[:,rows],wo_ref[...],0,0)
    c,r3=ln_stats(m2)
    xh3=c*r3
    n3=(xh3*g3_ref[...]+b3_ref[...]).astype(BF)
    n3_s[rows,:]=n3
    cot=split(cot_ref[...].reshape(FA,SB,D))
    cot_s[rows,:]=cot
    C=512
    GU=2
    @loop(FF//(C*GU),True)
    def _(o):
        cols=lambda q: pl.ds(mult((o*GU+q)*C,C),C)
        def up(q):
            return dg(n3,wu_ref[:,cols(q)],1,0)+bu_ref[:,cols(q)],dg(cot,wd_ref[cols(q),:],1,1)
        def gelu(q,pd):
            P,ph=phi_pair(pd[0])
            gp=((P+pd[0]*ph)*pd[1]).astype(BF)
            return (pd[0]*P).astype(BF),gp
        def keep(q,act,gp):
            act_s[rows,cols(q)]=act
            gp_s[rows,cols(q)]=gp
            vec_s[pl.ds(5+o*GU+q,1)]+=jnp.sum(gp.astype(F32),axis=0,keepdims=True)
        staged(GU,1,up,gelu,keep)
    out=m2+dg(act_s[rows,:],wd_ref[...],1,0)+bd_ref[...]
    out=out.astype(BF)
    if t==0:
        join(out,rows_ref,1)
    else:
        join(out,out_ref,0)
    dn3=dg(gp_s[rows,:],wu_ref[...],1,1)
    dg3=jnp.sum(dn3*xh3,axis=0,keepdims=True)
    db3=jnp.sum(dn3,axis=0,keepdims=True)
    cotf=cot.astype(F32)
    gm2=cotf+ln_back(dn3,xh3,r3,g3_ref[...])
    rr=gm2.astype(BF)
    r_s[rows,:]=rr
    dot_s[...]=dg(wo_ref[...],rr,1,1)
    @loop(NG,False)
    def _(g):
        gs,ps=group(g)
        flip=flipper(k_s,gs)
        def first(h):
            rl=rl_s[g,h:h+1]
            do=dot_s[head(h),gs]
            dd=jnp.sum(do*ht_s[head(h),ps].astype(F32),axis=0,keepdims=True)*rl
            dob=(do*rl).astype(BF)
            d3=[-z.astype(F32) for z in split3(dd)]
            return dob,dg(jnp.concatenate([v_s[gs,pair(h)],vb],axis=1),pad_head(dob,h%2,row_block(d3,G)),1,0)
        def second(h,dd):
            e=e_s[g*H+h]
            return dd[0],e,(e.astype(F32)*dd[1]).astype(BF)
        def third(h,dob,e,ds):
            dpt_s[2*D+h*64:2*D+h*64+64,ps]=dg(dob,e,1,1).astype(BF)
            dpt_s[D+h*64:D+h*64+64,ps]=(dg(qt_s[head(h),gs],ds,1,1)*LN2).astype(BF)
            dpt_s[head(h),ps]=(dg(flip(h),ds,1,0)*0.125).astype(BF)
        staged(H,2,first,second,third)
    dn2=dg(dpt_s[:,rows],w_ref[...],0,1).astype(BF).astype(F32)
    dg2=jnp.sum(dn2*xh2,axis=0,keepdims=True)
    db2=jnp.sum(dn2,axis=0,keepdims=True)
    gm=(gm2+ln_back(dn2,xh2,r2,g2_ref[...])).astype(BF)
    join(gm,rows_ref if t==0 else gm_ref,0)
    small=[dg2,db2,dg3,db3,jnp.sum(cotf,axis=0,keepdims=True)]
    for j,z in enumerate(small):
        vec_s[j:j+1]+=z
    @pl.when(i==last)
    def _():
        rp=D//nd; fp=FF//nd; nq=FF//D
        if t==0:
            emit=lambda at,acc: put_all(gr_ref,at,acc)
        else:
            prev.wait()
            core=cnt_ref[cnt_ref.shape[0]-1]%2
            emit=lambda at,acc: put(mine_ref,oth_ref,core,at,acc,prev_ref)
        base=nq*rp
        block=lambda q: pl.ds(mult(q*D,D),D)
        lines=lambda at: pl.ds(mult(at,rp),rp)
        @loop(nq,True)
        def _(q):
            emit(lines(q*rp),dg(n3_s[...],gp_s[:,block(q)],0,0))
            acc=dg(act_s[:,block(q)],cot_s[...],0,0)
            n=D//fp
            for j in range(n//2):
                even=acc[2*j*fp:(2*j+1)*fp]; odd=acc[(2*j+1)*fp:(2*j+2)*fp]
                c=q*(n//2)+j
                if t==0:
                    gr_ref[2*c,base:base+fp]=even.astype(BF)
                    gr_ref[2*c+1,base:base+fp]=odd.astype(BF)
                else:
                    even=even+prev_ref[2*c,base:base+fp].astype(F32)
                    odd=odd+prev_ref[2*c+1,base:base+fp].astype(F32)
                    mine_ref[c,base:base+fp]=jnp.where(core==0,even,odd).astype(BF)
                    oth_ref[c,base:base+fp]=jnp.where(core==0,odd,even).astype(BF)
        base2=base+fp
        @loop(3,True)
        def _(q):
            emit(lines(base2+q*rp),dg(n2_s[...],dpt_s[block(q),:],0,1))
        emit(lines(base2+3*rp),dg(ht_s[...],r_s[...],1,0))

def run_b(t, cnt, m, cot, ck, g2,b2,w,wo,g3,b3,wu,bu,wd,bd, prev=None, SB=32):
    nd,_,F,SL,D=cot.shape; FF=wu.shape[1]; R=nd*F*SB; N=nd*F*SL; G=nd*F*16
    rw=(4+FF//D)*(D//nd)+FF//nd
    row=lambda kinds,k: pl.BlockSpec((nd,kinds,F,SB,D),lambda i,s:(0,k,0,i,0))
    one=lambda *sh: pl.BlockSpec(sh,lambda i,s:(0,)*len(sh),pipeline_mode=pl.Buffered(1))
    con=lambda *sh: pl.BlockSpec(sh,lambda i,s:(0,)*len(sh))
    r=lambda z:z.reshape(1,-1)
    sd=jax.ShapeDtypeStruct
    pieces=isinstance(m,(list,tuple))
    ms=list(m) if pieces else [m]
    in_specs=[pl.BlockSpec((F,SB,D),lambda i,s:(0,i,0))]*nd if pieces else [row(1,0)]
    in_specs+=[row(1,ck),one(1,D),one(1,D),one(D,3*D),one(D,D),one(1,D),one(1,D),one(D,FF),one(1,FF),one(FF,D),one(1,D)]
    args=[cnt,*ms,cot,r(g2),r(b2),w,wo,r(g3),r(b3),wu,r(bu),wd,r(bd)]
    scratch=[pltpu.VMEM((N,D),BF),pltpu.VMEM((N,D),BF),pltpu.VMEM((N,D),BF),pltpu.VMEM((D,N),BF),pltpu.VMEM((3*D,N),BF),
             pltpu.VMEM((N,FF),BF),pltpu.VMEM((N,FF),BF),pltpu.VMEM((N,D),BF),
             pltpu.VMEM((D,R),BF),pltpu.VMEM((R,D),BF),pltpu.VMEM((R,D),BF),pltpu.VMEM((D//64*(SB//16),G,G),BF),pltpu.VMEM((R,D),F32),pltpu.VMEM((SB//16,8,G),F32),pltpu.VMEM((D,R),F32)]
    if t==0:
        out_specs=[row(2,0),con(nd,rw,D)]; out_shape=[sd((nd,2,F,SL,D),BF),sd((nd,rw,D),BF)]
    else:
        in_specs.append(pl.BlockSpec(memory_space=pl.ANY)); args.append(prev)
        out_specs=[row(1,0),row(1,0),con(nd//2,rw,D),con(nd//2,rw,D)]
        out_shape=[sd((nd,1,F,SL,D),BF)]*2+[sd((nd//2,rw,D),BF)]*2
        scratch+=[pltpu.VMEM((nd,rw,D),BF),pltpu.SemaphoreType.DMA]
    out_specs.append(pl.BlockSpec((16,D),lambda i,s:(0,0))); out_shape.append(sd((16,D),F32))
    gs=pltpu.PrefetchScalarGridSpec(num_scalar_prefetch=1,grid=(SL//SB,),in_specs=in_specs,out_specs=out_specs,scratch_shapes=scratch)
    return pl.pallas_call(partial(b_kernel,t,SB,len(ms)),grid_spec=gs,out_shape=out_shape,
        compiler_params=pltpu.CompilerParams(vmem_limit_bytes=62<<20),name="middle",
        cost_estimate=pl.CostEstimate(flops=2_000_000_000,bytes_accessed=1<<20,transcendentals=0))(*args)

from jax.sharding import PartitionSpec as P


def gather_sum(pieces):
    total=pieces[0].astype(F32)
    for z in pieces[1:]:
        total=total+z.astype(F32)
    return total

def pick(a,i,axis=0):
    return lax.dynamic_index_in_dim(a,i,axis,keepdims=False)

def swap_core(mine,oth):
    n=lax.axis_size("feat")
    return [mine,lax.ppermute(oth,"feat",[(i,i^1) for i in range(n)])]

def swap_task(s):
    nt=lax.axis_size("task"); t=lax.axis_index("task")
    nz,rw,D=s.shape
    s=s.reshape(nz,nt,rw//nt,D)
    return [pick(s,t,1)]+[lax.ppermute(pick(s,t^r,1),"task",[(i,i^r) for i in range(nt)]) for r in range(1,nt)]

def swap_chips(s):
    nf=lax.axis_size("feat"); z=lax.axis_index("feat")//2
    return [pick(s,z)]+[lax.ppermute(pick(s,z^r),"feat",[(i,i^(2*r)) for i in range(nf)]) for r in range(1,nf//2)]

def gather_task(s):
    nt=lax.axis_size("task")
    return [s]+[lax.ppermute(s,"task",[(i,i^r) for i in range(nt)]) for r in range(1,nt)]

def total(pieces):
    return gather_sum(pieces).astype(BF)

def move(a):
    return lax.all_to_all(a,"feat",0,0)

def move_pieces(pieces):
    n=len(pieces)
    return [pieces[0]]+[lax.ppermute(pieces[r],"feat",[(i,i^r) for i in range(n)]) for r in range(1,n)]

def middle_plain(t,cnt,m,cot,g2,b2,w,wo,g3,b3,wu,bu,wd,bd):
    FA=m.shape[0]; D=m.shape[-1]; H=D//64
    mf=m.astype(F32)
    def norm(v,g,b):
        c,r=ln_stats(v)
        return c*r*g+b
    mm=lambda a,b: jnp.einsum("fsd,de->fse",a,b,preferred_element_type=F32)
    mt=lambda a,b: jnp.einsum("fse,de->fsd",a,b,preferred_element_type=F32)
    out_sum=lambda a,b: jnp.einsum("fsd,fse->de",a,b,preferred_element_type=F32).astype(BF)
    n2=norm(mf,g2,b2).astype(BF)
    q,k,v=[z[...,0,:,:] for z in jnp.split(mm(n2,w).astype(BF).reshape(m.shape[:2]+(3,H,64)),3,axis=2)]
    keep=jnp.arange(FA)<cnt[t]
    s=jnp.where(keep,jnp.einsum("qshe,kshe->shqk",q,k,preferred_element_type=F32)*0.125,-1e30)
    pr=jax.nn.softmax(s,axis=-1)
    h2=jnp.einsum("shqk,kshe->qshe",pr.astype(BF),v,preferred_element_type=F32).astype(BF).reshape(m.shape)
    m2=mf+mm(h2,wo)
    n3,back3=jax.vjp(norm,m2,g3,b3)
    n3=n3.astype(BF)
    pre=mm(n3,wu)+bu
    act,back=jax.vjp(partial(jax.nn.gelu,approximate=False),pre)
    act=act.astype(BF)
    out=(m2+mm(act,wd)+bd).astype(BF)
    gp=back(mt(cot,wd))[0].astype(BF)
    a,dg3,db3=back3(mt(gp,wu))
    gm2=cot.astype(F32)+a
    rr=gm2.astype(BF)
    do=mt(rr,wo).astype(BF).reshape(q.shape)
    dp=jnp.einsum("qshe,kshe->shqk",do,v,preferred_element_type=F32)
    ds=(pr*(dp-jnp.sum(pr*dp,axis=-1,keepdims=True))).astype(BF)
    dq=jnp.einsum("shqk,kshe->qshe",ds,k,preferred_element_type=F32)*0.125
    dk=jnp.einsum("shqk,qshe->kshe",ds,q,preferred_element_type=F32)*0.125
    dv=jnp.einsum("shqk,qshe->kshe",pr.astype(BF),do,preferred_element_type=F32)
    dpk=jnp.stack([dq,dk,dv],axis=2).reshape(m.shape[:2]+(3*D,)).astype(BF)
    _,back2=jax.vjp(norm,mf,g2,b2)
    a,dg2,db2=back2(mt(dpk,w).astype(BF).astype(F32))
    small=jnp.concatenate([jnp.stack([dg2,db2,dg3,db3,jnp.sum(cot.astype(F32),axis=(0,1))]),jnp.zeros((3,D),F32)])
    dbu=jnp.sum(gp.astype(F32),axis=(0,1))[None]
    return out,(gm2+a).astype(BF),out_sum(n2,dpk),out_sum(h2,rr),out_sum(n3,gp),out_sum(act,cot),small,dbu

def run_b_plain(t,cnt,m,cot,ck,*rest,prev=None):
    nd,_,F,SL,D=m.shape
    out,gm,dw,dwo,dwu,dwd,small,dbu=middle_plain(t,cnt,m[:,0].reshape(nd*F,SL,D),cot[:,ck].reshape(nd*F,SL,D),*rest)
    v=jnp.concatenate([small[:5],dbu.reshape(-1,D)])
    v=jnp.pad(v,((0,16-v.shape[0]),(0,0)))
    out=out.reshape(nd,1,F,SL,D); gm=gm.reshape(nd,1,F,SL,D)
    blocks=lambda a: a.reshape(nd,D//nd,a.shape[1]//D,D).swapaxes(1,2).reshape(nd,-1,D)
    g=jnp.concatenate([blocks(dwu),dwd.reshape(nd,-1,D),blocks(dw),blocks(dwo)],axis=1)
    if t==0:
        return jnp.concatenate([gm,out],axis=1),g,v
    g=total([g,prev]).reshape(nd//2,2,-1,D)
    core=cnt[-1]%2
    return gm,out,pick(g,core,1),pick(g,1-core,1),v

def tie(*a):
    return lax.optimization_barrier(a)

def after(a,*b):
    return lax.optimization_barrier((a,)+b)[0]

def body(x,cot,lens,cnt,g1,b1,w1,wo1,g2,b2,w2,wo2,g3,b3,wu,bu,wd,bd):
    T,F,S,D=x.shape
    FF=wu.shape[1]
    nf=lax.axis_size("feat"); nt=lax.axis_size("task"); f=lax.axis_index("feat")
    sl=S//nf; rp=D//nf; fp=FF//nf; nz=nf//2
    fused=F*nf*16<=256
    me=f.astype(jnp.int32).reshape(1)
    lens=jnp.concatenate([lens,me]); cnt=jnp.concatenate([cnt,me])
    cot0=move(cot[0].reshape(F,nf,sl,D).swapaxes(0,1)[:,None])
    mid0,save0=run_a(0,lens,x,None,g1,b1,w1,wo1,nf,fused)
    mid0=move_pieces(mid0) if fused else move(mid0)
    mid1,save1=run_a(1,lens,x,cot,g1,b1,w1,wo1,nf,False)
    mid0,cot0,mid1,save1=tie(mid0,cot0,mid1,save1)
    mid1=move(mid1)
    rest=(g2,b2,w2,wo2,g3,b3,wu,bu,wd,bd)
    middle=run_b if fused else run_b_plain
    rows0,gr,v0=middle(0,cnt,mid0,cot0,0,*rest)
    mid1,rows0,gr=tie(mid1,rows0,gr)
    rows0=move(rows0)
    gm1,out1,*ga,v1=middle(1,cnt,mid1,mid1,1,*rest,prev=gr)
    rows0,gm1,ga=tie(rows0,gm1,ga)
    a=swap_core(*ga)
    gm1=move(gm1)
    a=swap_task(total(a))
    dpt0,gr=run_c(0,lens,x,after(rows0,a[0]),g1,b1,wo1,*save0)
    dx,e0=run_e(0,x,rows0,dpt0,g1,w1)
    gm1,dx=tie(gm1,dx)
    out1=move(after(out1,gm1))
    dpt1,*gc=run_c(1,lens,x,gm1,g1,b1,wo1,*save1,prev=gr)
    dpt1,gc,a=tie(dpt1,gc,a)
    c=swap_core(*gc)
    a=swap_chips(after(total(a),gc[0]))
    c=swap_task(total(c))
    dx,e1=run_e(1,x,after(gm1,c[0],out1),dpt1,g1,w1,dx)
    c,a,e1=tie(c,a,e1)
    a=gather_task(total(a))
    v=jnp.concatenate([v0+v1,e0+e1]).astype(BF)
    v=total(swap_core(v,v))
    nv=v.shape[0]
    c=swap_chips(jnp.concatenate([total(c),jnp.broadcast_to(v[None],(nz,)+v.shape)],axis=1))
    out=run_out((rows0,after(out1,c[0])))
    c,out,a=tie(c,out,a)
    c=gather_task(total(c))
    km=a[0].shape[0]; kl=4*rp//nt
    up,down,qkv2,out2,qkv1,out1=run_finish(lax.axis_index("task").astype(jnp.int32).reshape(1),a,c,km,kl,rp,fp,FF)
    v=gather_sum([p[-nv:] for p in c])
    vec=lambda i: lax.dynamic_slice_in_dim(v[i],f*rp,rp)
    return (out,dx,vec(16),vec(17),qkv1,out1,vec(0),vec(1),qkv2,out2,
        vec(2),vec(3),up,lax.dynamic_slice_in_dim(v[5:5+FF//D].reshape(FF),f*fp,fp),down,vec(4))

def solution(mesh):
    rows=P("task","feat",None,None)
    mat=P("feat",None)
    return jax.shard_map(body,mesh=mesh,
        in_specs=(rows,rows,P("task"),P("task"))+(P(),)*14,
        out_specs=(rows,rows,P("feat"),P("feat"),mat,mat,P("feat"),P("feat"),mat,mat,P("feat"),P("feat"),mat,P("feat"),mat,P("feat")),
        check_vma=False)
```

```python
import math
from functools import partial
import jax, jax.numpy as jnp
from jax import lax
from jax.experimental import pallas as pl
from jax.experimental.pallas import tpu as pltpu
BF=jnp.bfloat16; F32=jnp.float32
EPS=1e-5
LOG2E=1.4426950408889634
QS=0.125*LOG2E

def dg(a,b,ca,cb):
    return lax.dot_general(a,b,(((ca,),(cb,)),((),())),preferred_element_type=F32)

def ln_stats(v):
    mean=jnp.mean(v,axis=-1,keepdims=True)
    c=v-mean
    var=jnp.mean(c*c,axis=-1,keepdims=True)
    return c, lax.rsqrt(var+EPS)

def split3(v):
    a=v.astype(BF); r=v-a.astype(F32)
    b=r.astype(BF); r=r-b.astype(F32)
    return a,b,r.astype(BF)

def pad_head(rows,u,aug):
    z=jnp.zeros_like(rows)
    return jnp.concatenate([rows,z,aug] if u==0 else [z,rows,aug],axis=0)

def lane_block(cols,n):
    lane=lax.broadcasted_iota(jnp.int32,(n,128),1)
    out=jnp.zeros((n,128),F32)
    for i,c in enumerate(cols):
        out=jnp.where(lane==i,c,out)
    return out.astype(BF)

def row_block(rows,n):
    sub=lax.broadcasted_iota(jnp.int32,(128,n),0)
    out=jnp.zeros((128,n),F32)
    for i,r in enumerate(rows):
        out=jnp.where(sub==i,r,out)
    return out.astype(BF)

def staged(n,ahead,first,second,third):
    got=[first(i) for i in range(min(ahead,n))]
    last=None
    for i in range(n):
        if i+ahead<n:
            got.append(first(i+ahead))
        if last is not None:
            third(*last)
        last=(i,*second(i,got[i]))
        got[i]=None
    third(*last)

def a_kernel(t, both, len_ref, x_ref, *refs):
    if both:
        cot_ref,refs=refs[0],refs[1:]
    g_ref, b_ref, w_ref, wo_ref, *mid_refs, qt_ref, k_ref, v_ref, ht_ref, l_ref, mid_s=refs
    S,D=x_ref.shape[2:]
    x=x_ref[0,0].astype(F32)
    c,r=ln_stats(x)
    n1=(c*r*g_ref[...]+b_ref[...]).astype(BF)
    qt_ref[0]=(dg(w_ref[:,0:D],n1,0,1)*QS).astype(BF)
    k_ref[0]=dg(n1,w_ref[:,D:2*D],1,0).astype(BF)
    v_ref[0]=dg(n1,w_ref[:,2*D:3*D],1,0).astype(BF)
    n=len_ref[t]
    ks=lax.broadcasted_iota(jnp.int32,(S,1),0)
    bias=jnp.where(ks<n,0.0,-1e30)
    kb=lane_block([bias],S)
    qa=row_block([jnp.ones((1,S),F32)],S)
    ones=jnp.ones((16,S),BF)
    H=D//64; C=256
    units=[(h,c) for h in range(H) for c in range(0,S,C)]
    def scores(n):
        h,c=units[n]; p=h//2
        kp=jnp.concatenate([k_ref[0,:,p*128:p*128+128],kb],axis=1)
        return dg(kp,pad_head(qt_ref[0,h*64:h*64+64,c:c+C],h%2,qa[:,c:c+C]),1,0)
    vts={}
    def finish(n,e,m):
        h,c=units[n]
        if h//2 not in vts:
            vts[h//2]=v_ref[0,:,h//2*128:h//2*128+128].T
        va=jnp.concatenate([vts[h//2][h%2*64:h%2*64+64],ones],axis=0)
        o=dg(va,e,1,0)
        l=o[64:65]
        ht_ref[0,h*64:h*64+64,c:c+C]=(o[:64]*(1.0/l)).astype(BF)
        l_ref[0,h:h+1,c:c+C]=m+jnp.log2(l)
    def weigh(n,s):
        m=jnp.max(s,axis=0,keepdims=True)
        return jnp.exp2(s-m).astype(BF),m
    staged(len(units),2,scores,weigh,finish)
    mid_s[...]=x+dg(ht_ref[0],wo_ref[...],0,0)
    if len(mid_refs)==1:
        mid_ref=mid_refs[0]; nd=mid_ref.shape[0]; sl=S//nd
        for j in range(nd):
            mid_ref[j,0,0]=mid_s[j*sl:(j+1)*sl].astype(BF)
            if both:
                mid_ref[j,1,0]=cot_ref[0,0,j*sl:(j+1)*sl,:]
    else:
        nd=len(mid_refs); sl=S//nd; me=len_ref[len_ref.shape[0]-1]
        for r in range(nd):
            mid_refs[r][0]=mid_s[pl.ds(pl.multiple_of((r^me)*sl,sl),sl)].astype(BF)

def run_a(t, lens, x, cot, g, b, w, wo, nd, pieces):
    T,F,S,D=x.shape
    both=cot is not None
    kinds=2 if both else 1
    row=pl.BlockSpec((1,1,S,D),lambda f,s:(t,f,0,0))
    one=lambda *sh: pl.BlockSpec(sh,lambda f,s:(0,)*len(sh),pipeline_mode=pl.Buffered(1))
    per=lambda *sh: pl.BlockSpec((1,)+sh,lambda f,s:(f,0,0))
    sd=jax.ShapeDtypeStruct
    if pieces:
        out_specs=[per(S//nd,D)]*nd; out_shape=[sd((F,S//nd,D),BF)]*nd
    else:
        out_specs=[pl.BlockSpec((nd,kinds,1,S//nd,D),lambda f,s:(0,0,f,0,0))]; out_shape=[sd((nd,kinds,F,S//nd,D),BF)]
    n=len(out_specs)
    gs=pltpu.PrefetchScalarGridSpec(num_scalar_prefetch=1,grid=(F,),
        in_specs=[row]*kinds+[one(1,D),one(1,D),one(D,3*D),one(D,D)],
        out_specs=out_specs+[per(D,S),per(S,D),per(S,D),per(D,S),per(D//64,S)],scratch_shapes=[pltpu.VMEM((S,D),F32)])
    o=pl.pallas_call(partial(a_kernel,t,both),grid_spec=gs,
        out_shape=out_shape+[sd((F,D,S),BF),sd((F,S,D),BF),sd((F,S,D),BF),sd((F,D,S),BF),sd((F,D//64,S),F32)],
        compiler_params=pltpu.CompilerParams(vmem_limit_bytes=60<<20),name="fwd_samples",
        cost_estimate=pl.CostEstimate(flops=2_000_000_000,bytes_accessed=1<<20,transcendentals=0))(
            lens,*([x,cot] if both else [x]),g.reshape(1,D),b.reshape(1,D),w,wo)
    return (o[:n] if pieces else o[0]),o[n:]

LN2=0.6931471805599453

def ln_back(dn,xh,r,gain):
    gd=dn*gain
    return r*(gd-jnp.mean(gd,axis=-1,keepdims=True)-xh*jnp.mean(gd*xh,axis=-1,keepdims=True))

def put(mine_ref,oth_ref,core,at,acc,prev_ref):
    half=mine_ref.shape[0]; rp=acc.shape[0]//(2*half)
    if isinstance(at,int):
        at=pl.ds(at,rp)
    for j in range(half):
        even=acc[2*j*rp:(2*j+1)*rp]; odd=acc[(2*j+1)*rp:(2*j+2)*rp]
        if prev_ref is not None:
            even=even+prev_ref[2*j,at].astype(F32); odd=odd+prev_ref[2*j+1,at].astype(F32)
        mine_ref[j,at]=jnp.where(core==0,even,odd).astype(BF)
        oth_ref[j,at]=jnp.where(core==0,odd,even).astype(BF)

def put_all(g_ref,at,acc):
    n=g_ref.shape[0]; rp=acc.shape[0]//n
    if isinstance(at,int):
        at=pl.ds(at,rp)
    for j in range(n):
        g_ref[j,at]=acc[j*rp:(j+1)*rp].astype(BF)

def put_vec(vec_ref,prev_ref,*refs):
    n=vec_ref.shape[0]
    vec=vec_ref[...]
    if prev_ref is not None:
        vec=vec+prev_ref[0,prev_ref.shape[1]-n:].astype(F32)
    vec=vec.astype(BF)
    for ref in refs:
        for j in range(ref.shape[0]):
            ref[j,ref.shape[1]-n:]=vec

def c_kernel(t, len_ref, x_ref, gm_ref, g_ref, b_ref, w_hbm, wo_ref, qt_ref, k_ref, v_ref, ht_ref, l_ref, *refs):
    S,D=x_ref.shape[2:]
    if t==0:
        dx_ref, gr_ref, dpt_ref, dot_ref, acc_ref, vec_ref, w_ref, sem=refs
    else:
        prev_hbm, _, dx_ref, mine_ref, oth_ref, dpt_ref, dot_ref, acc_ref, vec_ref, w_ref, sem, prev_ref=refs
    f=pl.program_id(0); last=pl.num_programs(0)-1
    copies=[pltpu.make_async_copy(w_hbm,w_ref,sem.at[0])]
    if t>0:
        copies.append(pltpu.make_async_copy(prev_hbm,prev_ref,sem.at[1]))
    @pl.when(f==0)
    def _():
        for z in copies:
            z.start()
    c,r=ln_stats(x_ref[0,0].astype(F32))
    xh=c*r
    n1=(xh*g_ref[...]+b_ref[...]).astype(BF)
    nd=gm_ref.shape[0]
    s_in=jnp.concatenate([gm_ref[j,0,0] for j in range(nd)],axis=0)
    dot_ref[...]=dg(wo_ref[...],s_in,1,1).astype(BF)
    n=len_ref[t]
    ks=lax.broadcasted_iota(jnp.int32,(S,1),0)
    bias=jnp.where(ks<n,0.0,-1e30)
    one=jnp.ones((S,1),F32)
    kb=lane_block([bias,one,one,one],S)
    vb=lane_block([one,one,one],S)
    oner=jnp.ones((1,S),F32)
    C=256
    units=[(h,c) for h in range(D//64) for c in range(0,S,C)]
    kts={}
    def first(n):
        h,c=units[n]; p=h//2
        kp=jnp.concatenate([k_ref[0,:,p*128:p*128+128],kb],axis=1)
        vp=jnp.concatenate([v_ref[0,:,p*128:p*128+128],vb],axis=1)
        hs=slice(h*64,h*64+64)
        do=dot_ref[hs,c:c+C]
        dd=jnp.sum(do.astype(F32)*ht_ref[0,hs,c:c+C].astype(F32),axis=0,keepdims=True)
        l3=[-z.astype(F32) for z in split3(l_ref[0,h:h+1,c:c+C])]
        d3=[-z.astype(F32) for z in split3(dd)]
        s=dg(kp,pad_head(qt_ref[0,hs,c:c+C],h%2,row_block([oner[:,:C]]+l3,C)),1,0)
        return s,dg(vp,pad_head(do,h%2,row_block(d3,C)),1,0)
    def second(n,sd):
        e=jnp.exp2(sd[0])
        return e.astype(BF),(e*sd[1]).astype(BF)
    def third(n,e,ds):
        h,c=units[n]
        hs=slice(h*64,h*64+64)
        if h//2 not in kts:
            kts[h//2]=k_ref[0,:,h//2*128:h//2*128+128].T
        dv=dg(dot_ref[hs,c:c+C],e,1,1)
        dk=dg(qt_ref[0,hs,c:c+C],ds,1,1)*LN2
        if C<S:
            if c==0:
                part[h]=(dv,dk)
            else:
                dv=dv+part[h][0]; dk=dk+part[h][1]
                if c+C<S: part[h]=(dv,dk)
        if c+C==S:
            dpt_ref[2*D+h*64:2*D+h*64+64,:]=dv.astype(BF)
            dpt_ref[D+h*64:D+h*64+64,:]=dk.astype(BF)
        dpt_ref[h*64:h*64+64,c:c+C]=(dg(kts[h//2][h%2*64:h%2*64+64],ds,1,0)*0.125).astype(BF)
    part={}
    staged(len(units),1,first,second,third)
    @pl.when(f==0)
    def _():
        for z in copies:
            z.wait()
    dn=dg(dpt_ref[...],w_ref[...],0,1)
    @pl.when(f==0)
    def _():
        vec_ref[...]=jnp.zeros_like(vec_ref)
    vec_ref[0:1]+=jnp.sum(dn*xh,axis=0,keepdims=True)
    vec_ref[1:2]+=jnp.sum(dn,axis=0,keepdims=True)
    dx_ref[0,0]=(s_in.astype(F32)+ln_back(dn,xh,r,g_ref[...])).astype(BF)
    grads=lambda i: dg(ht_ref[0],s_in,1,0) if i==3 else dg(n1,dpt_ref[i*D:i*D+D,:],0,1)
    @pl.when(f==0)
    def _():
        for i in range(4):
            acc_ref[i]=grads(i)
    @pl.when((f>0)&(f<last))
    def _():
        for i in range(4):
            acc_ref[i]+=grads(i)
    @pl.when(f==last)
    def _():
        rp=D//nd
        for i in range(4):
            if t==0:
                put_all(gr_ref,i*rp,acc_ref[i]+grads(i))
            else:
                put(mine_ref,oth_ref,len_ref[len_ref.shape[0]-1]%2,i*rp,acc_ref[i]+grads(i),prev_ref)
        if t==0:
            put_vec(vec_ref,None,gr_ref)
        else:
            put_vec(vec_ref,prev_ref,mine_ref,oth_ref)

def run_c(t, lens, x, gm, g, b, w, wo, qt, k, v, ht, l, prev=None):
    T,F,S,D=x.shape; nd=gm.shape[0]; rw=4*(D//nd)+32
    one=lambda *sh: pl.BlockSpec(sh,lambda f,s:(0,)*len(sh),pipeline_mode=pl.Buffered(1))
    con=lambda *sh: pl.BlockSpec(sh,lambda f,s:(0,)*len(sh))
    per=lambda *sh: pl.BlockSpec((1,)+sh,lambda f,s:(f,0,0))
    in_specs=[pl.BlockSpec((1,1,S,D),lambda f,s:(t,f,0,0)),
              pl.BlockSpec((nd,1,1,S//nd,D),lambda f,s:(0,0,f,0,0)),
              one(1,D),one(1,D),pl.BlockSpec(memory_space=pl.ANY),one(D,D),per(D,S),per(S,D),per(S,D),per(D,S),per(D//64,S)]
    args=[lens,x,gm,g.reshape(1,D),b.reshape(1,D),w,wo,qt,k,v,ht,l]
    sd=jax.ShapeDtypeStruct
    out_specs=[pl.BlockSpec((1,1,S,D),lambda f,s:(t,f,0,0))]
    out_shape=[sd((T,F,S,D),BF)]
    alias={}
    scratch=[pltpu.VMEM((3*D,S),BF),pltpu.VMEM((D,S),BF),pltpu.VMEM((4,D,D),F32),pltpu.VMEM((32,D),F32),pltpu.VMEM((D,3*D),BF),pltpu.SemaphoreType.DMA((2,))]
    if t==0:
        out_specs.append(con(nd,rw,D)); out_shape.append(sd((nd,rw,D),BF))
    else:
        out_specs+=[con(nd//2,rw,D)]*2; out_shape+=[sd((nd//2,rw,D),BF)]*2
        in_specs+=[pl.BlockSpec(memory_space=pl.ANY)]*2; args+=[prev[1],prev[0]]
        scratch.append(pltpu.VMEM((nd,rw,D),BF))
        alias={len(args)-1:0}
    gs=pltpu.PrefetchScalarGridSpec(num_scalar_prefetch=1,grid=(F,),in_specs=in_specs,out_specs=out_specs,
        scratch_shapes=scratch)
    return pl.pallas_call(partial(c_kernel,t),grid_spec=gs,out_shape=out_shape,input_output_aliases=alias,
        compiler_params=pltpu.CompilerParams(vmem_limit_bytes=60<<20),name="bwd_samples",
        cost_estimate=pl.CostEstimate(flops=2_000_000_000,bytes_accessed=1<<20,transcendentals=0))(*args)

def out_kernel(nt, *refs):
    ins,out_ref=refs[:nt],refs[nt]
    for t in range(nt):
        nd=ins[t].shape[0]; sl=ins[t].shape[3]
        for j in range(nd):
            out_ref[t,0,j*sl:(j+1)*sl,:]=ins[t][j,0,0]

def run_out(outs):
    nd,_,F,sl,D=outs[0].shape; T=len(outs)
    return pl.pallas_call(partial(out_kernel,T),grid=(F,),
        in_specs=[pl.BlockSpec((nd,1,1,sl,D),lambda f,k=o.shape[1]-1:(0,k,f,0,0)) for o in outs],
        out_specs=pl.BlockSpec((T,1,nd*sl,D),lambda f:(0,f,0,0)),out_shape=jax.ShapeDtypeStruct((T,F,nd*sl,D),BF),
        compiler_params=pltpu.CompilerParams(vmem_limit_bytes=40<<20),name="rows_in_order",
        cost_estimate=pl.CostEstimate(flops=0,bytes_accessed=1<<20,transcendentals=0))(*outs)

def finish_kernel(rp, fp, at_ref, *refs):
    nt=(len(refs)-16)//2
    mids,lates=refs[:nt],refs[nt:2*nt]
    up_ref,down_ref,qkv2_ref,out2_ref,qkv1_ref,out1_ref,*vec_refs,mid_s,late_s=refs[2*nt:]
    t=at_ref[0]; f=at_ref[1]; D=mid_s.shape[1]; nq=up_ref.shape[1]//D
    km=mids[0].shape[0]; kl=lates[0].shape[0]
    for r in range(nt):
        mid_s[pl.ds(pl.multiple_of((r^t)*km,8),km)]=mids[r][...].astype(F32)
        late_s[pl.ds(pl.multiple_of((r^t)*kl,8),kl)]=lates[r][...].astype(F32)
    for q in range(nq):
        up_ref[:,q*D:q*D+D]=mid_s[q*rp:q*rp+rp]
    b=nq*rp
    down_ref[...]=mid_s[b:b+fp]
    b+=fp
    for q in range(3):
        qkv2_ref[:,q*D:q*D+D]=mid_s[b+q*rp:b+q*rp+rp]
        qkv1_ref[:,q*D:q*D+D]=late_s[q*rp:q*rp+rp]
    out2_ref[...]=mid_s[b+3*rp:b+4*rp]
    out1_ref[...]=late_s[3*rp:4*rp]
    b+=4*rp
    part=lambda row,at: pltpu.roll(jnp.broadcast_to(row,(8,D)),D-at,1)[0:1]
    for ref,src,i in zip(vec_refs,(late_s,late_s,mid_s,mid_s,mid_s,mid_s,mid_s),(4*rp,4*rp+1,b,b+1,b+2,b+3,b+4)):
        ref[...]=part(src[i:i+1],f*rp)[:,0:rp]
    per=D//fp
    row=mid_s[b+5:b+6]
    for q in range(1,nq):
        row=jnp.where(f//per==q,mid_s[b+5+q:b+6+q],row)
    vec_refs[7][...]=part(row,f%per*fp)[:,0:fp]

def run_finish(t, f, mids, lates, rp, fp, FF):
    nt=len(mids); km,D=mids[0].shape; kl=lates[0].shape[0]
    v=pl.BlockSpec(memory_space=pltpu.VMEM)
    sd=lambda *s: jax.ShapeDtypeStruct(s,F32)
    o=pl.pallas_call(partial(finish_kernel,rp,fp),in_specs=[pl.BlockSpec(memory_space=pltpu.SMEM)]+[v]*(2*nt),out_specs=[v]*14,
        out_shape=[sd(rp,FF),sd(fp,D),sd(rp,3*D),sd(rp,D),sd(rp,3*D),sd(rp,D)]+[sd(1,rp)]*7+[sd(1,fp)],
        scratch_shapes=[pltpu.VMEM((nt*km,D),F32),pltpu.VMEM((nt*kl,D),F32)],
        compiler_params=pltpu.CompilerParams(vmem_limit_bytes=40<<20),name="grads_in_order",
        cost_estimate=pl.CostEstimate(flops=0,bytes_accessed=1<<20,transcendentals=0))(jnp.stack([t,f]),*mids,*lates)
    vs=[z.reshape(-1) for z in o[6:]]
    return (*o[:6],*vs[:6],vs[7],vs[6])


def phi_pair(v):
    a=jnp.abs(v)
    t=1.0/(1.0+(0.3275911*0.7071067811865476)*a)
    e=jnp.exp2(v*v*(-0.5*LOG2E))
    y=t*(0.5*0.254829592+t*(0.5*-0.284496736+t*(0.5*1.421413741+t*(0.5*-1.453152027+t*(0.5*1.061405429)))))
    y=y*e
    return jnp.where(v<0,y,1.0-y), e*0.3989422804014327

def loop(n,rolled):
    def run(f):
        if rolled and n>1:
            pl.loop(0,n)(f)
        else:
            for i in range(n):
                f(i)
    return run

def mult(v,n):
    return v if isinstance(v,int) else pl.multiple_of(v,n)

def b_kernel(t, SB, nm, cnt_ref, *refs):
    m_refs,refs=refs[:nm],refs[nm:]
    cot_ref, g2_ref, b2_ref, w_ref, wo_ref, g3_ref, b3_ref, wu_hbm, bu_ref, wd_hbm, bd_ref, *refs=refs
    nd,_,F,_,D=cot_ref.shape
    FA=nd*F; H=D//64; FF=wu_hbm.shape[1]
    if t==0:
        rows_ref,gr_hbm,*refs=refs
        gr_ref=refs[-1]; refs=refs[:-1]
        outs=((gr_ref,gr_hbm),)
    else:
        prev_hbm,gm_ref,out_ref,mine_hbm,oth_hbm,*refs=refs
        prev_ref,sem,mine_ref,oth_ref=refs[-4:]; refs=refs[:-4]
        outs=((mine_ref,mine_hbm),(oth_ref,oth_hbm))
    n2_s, n3_s, r_s, ht_s, dpt_s, act_s, gp_s, cot_s, qt_s, k_s, v_s, e_s, m_s, rl_s, dot_s, vec_s, wu_ref, wd_ref, wsem, osem=refs
    G=FA*16; NG=SB//16; R=G*NG
    i=pl.program_id(0); last=pl.num_programs(0)-1
    if t>0:
        prev=pltpu.make_async_copy(prev_hbm,prev_ref,sem)
        @pl.when(i==0)
        def _():
            prev.start()
    at=pl.multiple_of(i*R,R); rows=pl.ds(at,R)
    weights=[pltpu.make_async_copy(wu_hbm,wu_ref,wsem.at[0]),pltpu.make_async_copy(wd_hbm,wd_ref,wsem.at[1])]
    @pl.when(i==0)
    def _():
        for z in weights:
            z.start()
    split=lambda v: jnp.concatenate([v[:,g*16:g*16+16].reshape(-1,D) for g in range(NG)],axis=0)
    def join(v,ref,kind):
        for g in range(NG):
            ref[:,kind,:,g*16:g*16+16,:]=v[g*G:g*G+G].reshape(nd,F,16,D)
    if nm==1:
        m=split(m_refs[0][...].reshape(FA,SB,D).astype(F32))
    else:
        me=cnt_ref[cnt_ref.shape[0]-1]
        for r in range(nm):
            for g in range(NG):
                m_s[pl.ds(pl.multiple_of((r^me)*(F*16)+g*G,F*16),F*16)]=m_refs[r][:,g*16:g*16+16].reshape(F*16,D).astype(F32)
        m=m_s[...]
    c,r2=ln_stats(m)
    xh2=c*r2
    n2=(xh2*g2_ref[...]+b2_ref[...]).astype(BF)
    n2_s[rows,:]=n2
    qt_s[...]=(dg(w_ref[:,0:D],n2,0,1)*QS).astype(BF)
    k_s[...]=dg(n2,w_ref[:,D:2*D],1,0).astype(BF)
    v_s[...]=dg(n2,w_ref[:,2*D:3*D],1,0).astype(BF)
    n=cnt_ref[t]
    krow=lax.broadcasted_iota(jnp.int32,(G,128),0)
    lane=lax.broadcasted_iota(jnp.int32,(G,128),1)
    kb=jnp.where(lane==0,jnp.where(krow//16>=n,-1e30,0.0),jnp.where(lane-1==krow%16,-1e30,0.0)).astype(BF)
    vb=jnp.where(lane<3,1.0,0.0).astype(BF)
    qcol=lax.broadcasted_iota(jnp.int32,(128,G),1)
    sub=lax.broadcasted_iota(jnp.int32,(128,G),0)
    qa=jnp.where((sub==0)|((sub<=16)&(sub-1!=qcol%16)),1.0,0.0).astype(BF)
    ones=jnp.ones((16,G),BF)
    pair=lambda h: slice(h//2*128,h//2*128+128)
    head=lambda h: slice(h*64,h*64+64)
    def flipper(ref,gs):
        flips={}
        def flip(h):
            if h//2 not in flips:
                flips[h//2]=ref[gs,pair(h)].T
            return flips[h//2][h%2*64:h%2*64+64]
        return flip
    def group(g):
        return pl.ds(mult(g*G,G),G),pl.ds(pl.multiple_of(at+g*G,G),G)
    @loop(NG,False)
    def _(g):
        gs,ps=group(g)
        flip=flipper(v_s,gs)
        def first(h):
            return dg(jnp.concatenate([k_s[gs,pair(h)],kb],axis=1),pad_head(qt_s[head(h),gs],h%2,qa),1,0)
        def second(h,s):
            e=jnp.exp2(s-jnp.max(s,axis=0,keepdims=True)).astype(BF)
            e_s[g*H+h]=e
            return (e,)
        def third(h,e):
            o=dg(jnp.concatenate([flip(h),ones],axis=0),e,1,0)
            rl=1.0/o[64:65]
            rl_s[g,h:h+1]=rl
            ht_s[head(h),ps]=(o[:64]*rl).astype(BF)
        staged(H,2,first,second,third)
    @pl.when(i==0)
    def _():
        vec_s[...]=jnp.zeros_like(vec_s)
    m2=m+dg(ht_s[:,rows],wo_ref[...],0,0)
    c,r3=ln_stats(m2)
    xh3=c*r3
    n3=(xh3*g3_ref[...]+b3_ref[...]).astype(BF)
    n3_s[rows,:]=n3
    cot=split(cot_ref[...].reshape(FA,SB,D))
    cot_s[rows,:]=cot
    C=512
    @pl.when(i==0)
    def _():
        for z in weights:
            z.wait()
    GU=2
    @loop(FF//(C*GU),True)
    def _(o):
        cols=lambda q: pl.ds(mult((o*GU+q)*C,C),C)
        def up(q):
            return dg(n3,wu_ref[:,cols(q)],1,0)+bu_ref[:,cols(q)],dg(cot,wd_ref[cols(q),:],1,1)
        def gelu(q,pd):
            P,ph=phi_pair(pd[0])
            gp=((P+pd[0]*ph)*pd[1]).astype(BF)
            return (pd[0]*P).astype(BF),gp
        def keep(q,act,gp):
            act_s[rows,cols(q)]=act
            gp_s[rows,cols(q)]=gp
            vec_s[pl.ds(5+o*GU+q,1)]+=jnp.sum(gp.astype(F32),axis=0,keepdims=True)
        staged(GU,1,up,gelu,keep)
    out=m2+dg(act_s[rows,:],wd_ref[...],1,0)+bd_ref[...]
    out=out.astype(BF)
    if t==0:
        join(out,rows_ref,1)
    else:
        join(out,out_ref,0)
    dn3=dg(gp_s[rows,:],wu_ref[...],1,1)
    dg3=jnp.sum(dn3*xh3,axis=0,keepdims=True)
    db3=jnp.sum(dn3,axis=0,keepdims=True)
    cotf=cot.astype(F32)
    gm2=cotf+ln_back(dn3,xh3,r3,g3_ref[...])
    rr=gm2.astype(BF)
    r_s[rows,:]=rr
    dot_s[...]=dg(wo_ref[...],rr,1,1)
    @loop(NG,False)
    def _(g):
        gs,ps=group(g)
        flip=flipper(k_s,gs)
        def first(h):
            rl=rl_s[g,h:h+1]
            do=dot_s[head(h),gs]
            dd=jnp.sum(do*ht_s[head(h),ps].astype(F32),axis=0,keepdims=True)*rl
            dob=(do*rl).astype(BF)
            d3=[-z.astype(F32) for z in split3(dd)]
            return dob,dg(jnp.concatenate([v_s[gs,pair(h)],vb],axis=1),pad_head(dob,h%2,row_block(d3,G)),1,0)
        def second(h,dd):
            e=e_s[g*H+h]
            return dd[0],e,(e.astype(F32)*dd[1]).astype(BF)
        def third(h,dob,e,ds):
            dpt_s[2*D+h*64:2*D+h*64+64,ps]=dg(dob,e,1,1).astype(BF)
            dpt_s[D+h*64:D+h*64+64,ps]=(dg(qt_s[head(h),gs],ds,1,1)*LN2).astype(BF)
            dpt_s[head(h),ps]=(dg(flip(h),ds,1,0)*0.125).astype(BF)
        staged(H,2,first,second,third)
    dn2=dg(dpt_s[:,rows],w_ref[...],0,1).astype(BF).astype(F32)
    dg2=jnp.sum(dn2*xh2,axis=0,keepdims=True)
    db2=jnp.sum(dn2,axis=0,keepdims=True)
    gm=(gm2+ln_back(dn2,xh2,r2,g2_ref[...])).astype(BF)
    join(gm,rows_ref if t==0 else gm_ref,0)
    small=[dg2,db2,dg3,db3,jnp.sum(cotf,axis=0,keepdims=True)]
    for j,z in enumerate(small):
        vec_s[j:j+1]+=z
    @pl.when(i==last)
    def _():
        rp=D//nd; fp=FF//nd; nq=FF//D
        if t==0:
            emit=lambda at,acc: put_all(gr_ref,at,acc)
        else:
            prev.wait()
            core=cnt_ref[cnt_ref.shape[0]-1]%2
            emit=lambda at,acc: put(mine_ref,oth_ref,core,at,acc,prev_ref)
        base=nq*rp
        block=lambda q: pl.ds(mult(q*D,D),D)
        lines=lambda at: pl.ds(mult(at,rp),rp)
        @loop(nq,True)
        def _(q):
            emit(lines(q*rp),dg(n3_s[...],gp_s[:,block(q)],0,0))
            acc=dg(act_s[:,block(q)],cot_s[...],0,0)
            n=D//fp
            for j in range(n//2):
                even=acc[2*j*fp:(2*j+1)*fp]; odd=acc[(2*j+1)*fp:(2*j+2)*fp]
                c=q*(n//2)+j
                if t==0:
                    gr_ref[2*c,base:base+fp]=even.astype(BF)
                    gr_ref[2*c+1,base:base+fp]=odd.astype(BF)
                else:
                    even=even+prev_ref[2*c,base:base+fp].astype(F32)
                    odd=odd+prev_ref[2*c+1,base:base+fp].astype(F32)
                    mine_ref[c,base:base+fp]=jnp.where(core==0,even,odd).astype(BF)
                    oth_ref[c,base:base+fp]=jnp.where(core==0,odd,even).astype(BF)
        base2=base+fp
        first=[pltpu.make_async_copy(v.at[:,0:base2],h.at[:,0:base2],osem.at[2*k]) for k,(v,h) in enumerate(outs)]
        for z in first:
            z.start()
        @loop(3,True)
        def _(q):
            emit(lines(base2+q*rp),dg(n2_s[...],dpt_s[block(q),:],0,1))
        emit(lines(base2+3*rp),dg(ht_s[...],r_s[...],1,0))
        if t==0:
            put_vec(vec_s,None,gr_ref)
        else:
            put_vec(vec_s,prev_ref,mine_ref,oth_ref)
        rest=[pltpu.make_async_copy(v.at[:,base2:],h.at[:,base2:],osem.at[2*k+1]) for k,(v,h) in enumerate(outs)]
        for z in rest:
            z.start()
        for z in first+rest:
            z.wait()

def run_b(t, cnt, m, cot, ck, g2,b2,w,wo,g3,b3,wu,bu,wd,bd, prev=None, SB=32):
    nd,_,F,SL,D=cot.shape; FF=wu.shape[1]; R=nd*F*SB; N=nd*F*SL; G=nd*F*16
    rw=(4+FF//D)*(D//nd)+FF//nd+32
    row=lambda kinds,k: pl.BlockSpec((nd,kinds,F,SB,D),lambda i,s:(0,k,0,i,0))
    one=lambda *sh: pl.BlockSpec(sh,lambda i,s:(0,)*len(sh),pipeline_mode=pl.Buffered(1))
    hbm=pl.BlockSpec(memory_space=pl.ANY)
    r=lambda z:z.reshape(1,-1)
    sd=jax.ShapeDtypeStruct
    pieces=isinstance(m,(list,tuple))
    ms=list(m) if pieces else [m]
    in_specs=[pl.BlockSpec((F,SB,D),lambda i,s:(0,i,0))]*nd if pieces else [row(1,0)]
    in_specs+=[row(1,ck),one(1,D),one(1,D),one(D,3*D),one(D,D),one(1,D),one(1,D),hbm,one(1,FF),hbm,one(1,D)]
    args=[cnt,*ms,cot,r(g2),r(b2),w,wo,r(g3),r(b3),wu,r(bu),wd,r(bd)]
    scratch=[pltpu.VMEM((N,D),BF),pltpu.VMEM((N,D),BF),pltpu.VMEM((N,D),BF),pltpu.VMEM((D,N),BF),pltpu.VMEM((3*D,N),BF),
             pltpu.VMEM((N,FF),BF),pltpu.VMEM((N,FF),BF),pltpu.VMEM((N,D),BF),
             pltpu.VMEM((D,R),BF),pltpu.VMEM((R,D),BF),pltpu.VMEM((R,D),BF),pltpu.VMEM((D//64*(SB//16),G,G),BF),pltpu.VMEM((R,D),F32),pltpu.VMEM((SB//16,8,G),F32),pltpu.VMEM((D,R),F32),pltpu.VMEM((32,D),F32),
             pltpu.VMEM((D,FF),BF),pltpu.VMEM((FF,D),BF),pltpu.SemaphoreType.DMA((2,)),pltpu.SemaphoreType.DMA((4,))]
    if t==0:
        out_specs=[row(2,0),hbm]; out_shape=[sd((nd,2,F,SL,D),BF),sd((nd,rw,D),BF)]
        scratch.append(pltpu.VMEM((nd,rw,D),BF))
    else:
        in_specs.append(hbm); args.append(prev)
        out_specs=[row(1,0),row(1,0),hbm,hbm]
        out_shape=[sd((nd,1,F,SL,D),BF)]*2+[sd((nd//2,rw,D),BF)]*2
        scratch+=[pltpu.VMEM((nd,rw,D),BF),pltpu.SemaphoreType.DMA,pltpu.VMEM((nd//2,rw,D),BF),pltpu.VMEM((nd//2,rw,D),BF)]
    gs=pltpu.PrefetchScalarGridSpec(num_scalar_prefetch=1,grid=(SL//SB,),in_specs=in_specs,out_specs=out_specs,scratch_shapes=scratch)
    return pl.pallas_call(partial(b_kernel,t,SB,len(ms)),grid_spec=gs,out_shape=out_shape,
        compiler_params=pltpu.CompilerParams(vmem_limit_bytes=62<<20),name="middle",
        cost_estimate=pl.CostEstimate(flops=2_000_000_000,bytes_accessed=1<<20,transcendentals=0))(*args)

from jax.sharding import PartitionSpec as P


def gather_sum(pieces):
    total=pieces[0].astype(F32)
    for z in pieces[1:]:
        total=total+z.astype(F32)
    return total

def pick(a,i,axis=0):
    return lax.dynamic_index_in_dim(a,i,axis,keepdims=False)

def swap_core(mine,oth):
    n=lax.axis_size("feat")
    return [mine,lax.ppermute(oth,"feat",[(i,i^1) for i in range(n)])]

def swap_task(s):
    nt=lax.axis_size("task"); t=lax.axis_index("task")
    nz,rw,D=s.shape
    s=s.reshape(nz,nt,rw//nt,D)
    return [pick(s,t,1)]+[lax.ppermute(pick(s,t^r,1),"task",[(i,i^r) for i in range(nt)]) for r in range(1,nt)]

def swap_chips(s):
    nf=lax.axis_size("feat"); z=lax.axis_index("feat")//2
    return [pick(s,z)]+[lax.ppermute(pick(s,z^r),"feat",[(i,i^(2*r)) for i in range(nf)]) for r in range(1,nf//2)]

def halve_chips(s,bit):
    nf=lax.axis_size("feat"); b=lax.axis_index("feat")//(2*bit)%2
    s=s.reshape(s.shape[0]//2,2,*s.shape[1:])
    return [pick(s,b,1),lax.ppermute(pick(s,1-b,1),"feat",[(i,i^(2*bit)) for i in range(nf)])]

def gather_task(s):
    nt=lax.axis_size("task")
    return [s]+[lax.ppermute(s,"task",[(i,i^r) for i in range(nt)]) for r in range(1,nt)]

def total(pieces):
    return gather_sum(pieces).astype(BF)

def move(a):
    return lax.all_to_all(a,"feat",0,0)

def move_pieces(pieces):
    n=len(pieces)
    return [pieces[0]]+[lax.ppermute(pieces[r],"feat",[(i,i^r) for i in range(n)]) for r in range(1,n)]

def middle_plain(t,cnt,m,cot,g2,b2,w,wo,g3,b3,wu,bu,wd,bd):
    FA=m.shape[0]; D=m.shape[-1]; H=D//64
    mf=m.astype(F32)
    def norm(v,g,b):
        c,r=ln_stats(v)
        return c*r*g+b
    mm=lambda a,b: jnp.einsum("fsd,de->fse",a,b,preferred_element_type=F32)
    mt=lambda a,b: jnp.einsum("fse,de->fsd",a,b,preferred_element_type=F32)
    out_sum=lambda a,b: jnp.einsum("fsd,fse->de",a,b,preferred_element_type=F32).astype(BF)
    n2=norm(mf,g2,b2).astype(BF)
    q,k,v=[z[...,0,:,:] for z in jnp.split(mm(n2,w).astype(BF).reshape(m.shape[:2]+(3,H,64)),3,axis=2)]
    keep=jnp.arange(FA)<cnt[t]
    s=jnp.where(keep,jnp.einsum("qshe,kshe->shqk",q,k,preferred_element_type=F32)*0.125,-1e30)
    pr=jax.nn.softmax(s,axis=-1)
    h2=jnp.einsum("shqk,kshe->qshe",pr.astype(BF),v,preferred_element_type=F32).astype(BF).reshape(m.shape)
    m2=mf+mm(h2,wo)
    n3,back3=jax.vjp(norm,m2,g3,b3)
    n3=n3.astype(BF)
    pre=mm(n3,wu)+bu
    act,back=jax.vjp(partial(jax.nn.gelu,approximate=False),pre)
    act=act.astype(BF)
    out=(m2+mm(act,wd)+bd).astype(BF)
    gp=back(mt(cot,wd))[0].astype(BF)
    a,dg3,db3=back3(mt(gp,wu))
    gm2=cot.astype(F32)+a
    rr=gm2.astype(BF)
    do=mt(rr,wo).astype(BF).reshape(q.shape)
    dp=jnp.einsum("qshe,kshe->shqk",do,v,preferred_element_type=F32)
    ds=(pr*(dp-jnp.sum(pr*dp,axis=-1,keepdims=True))).astype(BF)
    dq=jnp.einsum("shqk,kshe->qshe",ds,k,preferred_element_type=F32)*0.125
    dk=jnp.einsum("shqk,qshe->kshe",ds,q,preferred_element_type=F32)*0.125
    dv=jnp.einsum("shqk,qshe->kshe",pr.astype(BF),do,preferred_element_type=F32)
    dpk=jnp.stack([dq,dk,dv],axis=2).reshape(m.shape[:2]+(3*D,)).astype(BF)
    _,back2=jax.vjp(norm,mf,g2,b2)
    a,dg2,db2=back2(mt(dpk,w).astype(BF).astype(F32))
    small=jnp.concatenate([jnp.stack([dg2,db2,dg3,db3,jnp.sum(cot.astype(F32),axis=(0,1))]),jnp.zeros((3,D),F32)])
    dbu=jnp.sum(gp.astype(F32),axis=(0,1))[None]
    return out,(gm2+a).astype(BF),out_sum(n2,dpk),out_sum(h2,rr),out_sum(n3,gp),out_sum(act,cot),small,dbu

def run_b_plain(t,cnt,m,cot,ck,*rest,prev=None):
    nd,_,F,SL,D=m.shape
    out,gm,dw,dwo,dwu,dwd,small,dbu=middle_plain(t,cnt,m[:,0].reshape(nd*F,SL,D),cot[:,ck].reshape(nd*F,SL,D),*rest)
    v=jnp.concatenate([small[:5],dbu.reshape(-1,D)])
    v=jnp.pad(v,((0,32-v.shape[0]),(0,0))).astype(BF)
    out=out.reshape(nd,1,F,SL,D); gm=gm.reshape(nd,1,F,SL,D)
    blocks=lambda a: a.reshape(nd,D//nd,a.shape[1]//D,D).swapaxes(1,2).reshape(nd,-1,D)
    g=jnp.concatenate([blocks(dwu),dwd.reshape(nd,-1,D),blocks(dw),blocks(dwo),jnp.broadcast_to(v[None],(nd,)+v.shape)],axis=1)
    if t==0:
        return jnp.concatenate([gm,out],axis=1),g
    g=total([g,prev]).reshape(nd//2,2,-1,D)
    core=cnt[-1]%2
    return gm,out,pick(g,core,1),pick(g,1-core,1)

def tie(*a):
    return lax.optimization_barrier(a)

def after(a,*b):
    return lax.optimization_barrier((a,)+b)[0]

def body(x,cot,lens,cnt,g1,b1,w1,wo1,g2,b2,w2,wo2,g3,b3,wu,bu,wd,bd):
    T,F,S,D=x.shape
    FF=wu.shape[1]
    nf=lax.axis_size("feat"); nt=lax.axis_size("task"); f=lax.axis_index("feat")
    sl=S//nf; rp=D//nf; fp=FF//nf; nz=nf//2
    fused=F*nf*16<=256
    me=f.astype(jnp.int32).reshape(1)
    lens=jnp.concatenate([lens,me]); cnt=jnp.concatenate([cnt,me])
    cot0=move(cot[0].reshape(F,nf,sl,D).swapaxes(0,1)[:,None])
    mid0,save0=run_a(0,lens,x,None,g1,b1,w1,wo1,nf,fused)
    mid0=move_pieces(mid0) if fused else move(mid0)
    mid1,save1=run_a(1,lens,x,cot,g1,b1,w1,wo1,nf,False)
    if fused:
        mid0,cot0,mid1,save1=tie(mid0,cot0,mid1,save1)
    mid1=move(mid1)
    rest=(g2,b2,w2,wo2,g3,b3,wu,bu,wd,bd)
    middle=run_b if fused else run_b_plain
    rows0,gr=middle(0,cnt,mid0,cot0,0,*rest)
    mid1,rows0,gr=tie(mid1,rows0,gr)
    rows0=move(rows0)
    gm1,out1,*ga=middle(1,cnt,mid1,mid1,1,*rest,prev=gr)
    rows0,gm1,ga=tie(rows0,gm1,ga)
    a=swap_core(*ga)
    gm1=move(gm1)
    a=swap_task(total(a))
    dx,gr=run_c(0,lens,x,after(rows0,a[0]),g1,b1,w1,wo1,*save0)
    gm1,dx=tie(gm1,dx)
    out1=move(after(out1,gm1))
    dx,*gc=run_c(1,lens,x,gm1,g1,b1,w1,wo1,*save1,prev=(dx,gr))
    gc,a=tie(gc,a)
    c=swap_core(*gc)
    a=halve_chips(after(total(a),gc[0]),1)
    c,out1=tie(c,out1)
    c=swap_task(total(c))
    a,c[0]=tie(a,c[0])
    bit=2
    while bit<nz:
        a=halve_chips(total(a),bit)
        bit*=2
    out=run_out((rows0,after(out1,a[0])))
    c,out=tie(c,out)
    c=swap_chips(total(c))
    a,c[0]=tie(a,c[0])
    a=gather_task(total(a)[0])
    c=gather_task(total(c))
    up,down,qkv2,out2,qkv1,out1,*vs=run_finish(lax.axis_index("task").astype(jnp.int32),f.astype(jnp.int32),a,c,rp,fp,FF)
    return (out,dx,vs[0],vs[1],qkv1,out1,vs[2],vs[3],qkv2,out2,vs[4],vs[5],up,vs[6],down,vs[7])

def solution(mesh):
    rows=P("task","feat",None,None)
    mat=P("feat",None)
    return jax.shard_map(body,mesh=mesh,
        in_specs=(rows,rows,P("task"),P("task"))+(P(),)*14,
        out_specs=(rows,rows,P("feat"),P("feat"),mat,mat,P("feat"),P("feat"),mat,mat,P("feat"),P("feat"),mat,P("feat"),mat,P("feat")),
        check_vma=False)
```

```python
import math
from functools import partial
import jax, jax.numpy as jnp
from jax import lax
from jax.experimental import pallas as pl
from jax.experimental.pallas import tpu as pltpu
BF=jnp.bfloat16; F32=jnp.float32
EPS=1e-5
LOG2E=1.4426950408889634
QS=0.125*LOG2E

def dg(a,b,ca,cb):
    return lax.dot_general(a,b,(((ca,),(cb,)),((),())),preferred_element_type=F32)

def ln_stats(v):
    mean=jnp.mean(v,axis=-1,keepdims=True)
    c=v-mean
    var=jnp.mean(c*c,axis=-1,keepdims=True)
    return c, lax.rsqrt(var+EPS)

def split3(v):
    a=v.astype(BF); r=v-a.astype(F32)
    b=r.astype(BF); r=r-b.astype(F32)
    return a,b,r.astype(BF)

def pad_head(rows,u,aug):
    z=jnp.zeros_like(rows)
    return jnp.concatenate([rows,z,aug] if u==0 else [z,rows,aug],axis=0)

def lane_block(cols,n):
    lane=lax.broadcasted_iota(jnp.int32,(n,128),1)
    out=jnp.zeros((n,128),F32)
    for i,c in enumerate(cols):
        out=jnp.where(lane==i,c,out)
    return out.astype(BF)

def row_block(rows,n):
    sub=lax.broadcasted_iota(jnp.int32,(128,n),0)
    out=jnp.zeros((128,n),F32)
    for i,r in enumerate(rows):
        out=jnp.where(sub==i,r,out)
    return out.astype(BF)

def staged(n,ahead,first,second,third):
    got=[first(i) for i in range(min(ahead,n))]
    last=None
    for i in range(n):
        if i+ahead<n:
            got.append(first(i+ahead))
        if last is not None:
            third(*last)
        last=(i,*second(i,got[i]))
        got[i]=None
    third(*last)

def a_kernel(t, both, len_ref, x_ref, *refs):
    if both:
        cot_ref,refs=refs[0],refs[1:]
    g_ref, b_ref, w_ref, wo_ref, *mid_refs, qt_ref, k_ref, v_ref, ht_ref, l_ref, mid_s=refs
    S,D=x_ref.shape[2:]
    x=x_ref[0,0].astype(F32)
    c,r=ln_stats(x)
    n1=(c*r*g_ref[...]+b_ref[...]).astype(BF)
    qt_ref[0]=(dg(w_ref[:,0:D],n1,0,1)*QS).astype(BF)
    k_ref[0]=dg(n1,w_ref[:,D:2*D],1,0).astype(BF)
    v_ref[0]=dg(n1,w_ref[:,2*D:3*D],1,0).astype(BF)
    n=len_ref[t]
    ks=lax.broadcasted_iota(jnp.int32,(S,1),0)
    bias=jnp.where(ks<n,0.0,-1e30)
    kb=lane_block([bias],S)
    qa=row_block([jnp.ones((1,S),F32)],S)
    ones=jnp.ones((16,S),BF)
    H=D//64; C=256
    units=[(h,c) for h in range(H) for c in range(0,S,C)]
    def scores(n):
        h,c=units[n]; p=h//2
        kp=jnp.concatenate([k_ref[0,:,p*128:p*128+128],kb],axis=1)
        return dg(kp,pad_head(qt_ref[0,h*64:h*64+64,c:c+C],h%2,qa[:,c:c+C]),1,0)
    vts={}
    def finish(n,e,m):
        h,c=units[n]
        if h//2 not in vts:
            vts[h//2]=v_ref[0,:,h//2*128:h//2*128+128].T
        va=jnp.concatenate([vts[h//2][h%2*64:h%2*64+64],ones],axis=0)
        o=dg(va,e,1,0)
        l=o[64:65]
        ht_ref[0,h*64:h*64+64,c:c+C]=(o[:64]*(1.0/l)).astype(BF)
        l_ref[0,h:h+1,c:c+C]=m+jnp.log2(l)
    def weigh(n,s):
        m=jnp.max(s,axis=0,keepdims=True)
        return jnp.exp2(s-m).astype(BF),m
    staged(len(units),2,scores,weigh,finish)
    mid_s[...]=x+dg(ht_ref[0],wo_ref[...],0,0)
    if len(mid_refs)==1:
        mid_ref=mid_refs[0]; nd=mid_ref.shape[0]; sl=S//nd
        for j in range(nd):
            mid_ref[j,0,0]=mid_s[j*sl:(j+1)*sl].astype(BF)
            if both:
                mid_ref[j,1,0]=cot_ref[0,0,j*sl:(j+1)*sl,:]
    else:
        nd=len(mid_refs); sl=S//nd; me=len_ref[len_ref.shape[0]-1]
        for r in range(nd):
            mid_refs[r][0]=mid_s[pl.ds(pl.multiple_of((r^me)*sl,sl),sl)].astype(BF)

def run_a(t, lens, x, cot, g, b, w, wo, nd, pieces):
    T,F,S,D=x.shape
    both=cot is not None
    kinds=2 if both else 1
    row=pl.BlockSpec((1,1,S,D),lambda f,s:(t,f,0,0))
    one=lambda *sh: pl.BlockSpec(sh,lambda f,s:(0,)*len(sh),pipeline_mode=pl.Buffered(1))
    per=lambda *sh: pl.BlockSpec((1,)+sh,lambda f,s:(f,0,0))
    sd=jax.ShapeDtypeStruct
    if pieces:
        out_specs=[per(S//nd,D)]*nd; out_shape=[sd((F,S//nd,D),BF)]*nd
    else:
        out_specs=[pl.BlockSpec((nd,kinds,1,S//nd,D),lambda f,s:(0,0,f,0,0))]; out_shape=[sd((nd,kinds,F,S//nd,D),BF)]
    n=len(out_specs)
    gs=pltpu.PrefetchScalarGridSpec(num_scalar_prefetch=1,grid=(F,),
        in_specs=[row]*kinds+[one(1,D),one(1,D),one(D,3*D),one(D,D)],
        out_specs=out_specs+[per(D,S),per(S,D),per(S,D),per(D,S),per(D//64,S)],scratch_shapes=[pltpu.VMEM((S,D),F32)])
    o=pl.pallas_call(partial(a_kernel,t,both),grid_spec=gs,
        out_shape=out_shape+[sd((F,D,S),BF),sd((F,S,D),BF),sd((F,S,D),BF),sd((F,D,S),BF),sd((F,D//64,S),F32)],
        compiler_params=pltpu.CompilerParams(vmem_limit_bytes=60<<20),name="fwd_samples",
        cost_estimate=pl.CostEstimate(flops=2_000_000_000,bytes_accessed=1<<20,transcendentals=0))(
            lens,*([x,cot] if both else [x]),g.reshape(1,D),b.reshape(1,D),w,wo)
    return (o[:n] if pieces else o[0]),o[n:]

LN2=0.6931471805599453

def ln_back(dn,xh,r,gain):
    gd=dn*gain
    return r*(gd-jnp.mean(gd,axis=-1,keepdims=True)-xh*jnp.mean(gd*xh,axis=-1,keepdims=True))

def put(mine_ref,oth_ref,core,at,acc,prev_ref):
    half=mine_ref.shape[0]; rp=acc.shape[0]//(2*half)
    if isinstance(at,int):
        at=pl.ds(at,rp)
    for j in range(half):
        even=acc[2*j*rp:(2*j+1)*rp]; odd=acc[(2*j+1)*rp:(2*j+2)*rp]
        if prev_ref is not None:
            even=even+prev_ref[2*j,at].astype(F32); odd=odd+prev_ref[2*j+1,at].astype(F32)
        mine_ref[j,at]=jnp.where(core==0,even,odd).astype(BF)
        oth_ref[j,at]=jnp.where(core==0,odd,even).astype(BF)

def put_all(g_ref,at,acc):
    n=g_ref.shape[0]; rp=acc.shape[0]//n
    if isinstance(at,int):
        at=pl.ds(at,rp)
    for j in range(n):
        g_ref[j,at]=acc[j*rp:(j+1)*rp].astype(BF)

def put_vec(vec_ref,prev_ref,*refs):
    n=vec_ref.shape[0]
    vec=vec_ref[...]
    if prev_ref is not None:
        vec=vec+prev_ref[0,prev_ref.shape[1]-n:].astype(F32)
    vec=vec.astype(BF)
    for ref in refs:
        for j in range(ref.shape[0]):
            ref[j,ref.shape[1]-n:]=vec

def c_kernel(t, len_ref, x_ref, gm_ref, g_ref, b_ref, w_hbm, wo_ref, qt_ref, k_ref, v_ref, ht_ref, l_ref, *refs):
    S,D=x_ref.shape[2:]
    if t==0:
        dx_ref, gr_ref, dpt_ref, dot_ref, acc_ref, vec_ref, w_ref, sem=refs
    else:
        prev_hbm, _, dx_ref, mine_ref, oth_ref, dpt_ref, dot_ref, acc_ref, vec_ref, w_ref, sem, prev_ref=refs
    f=pl.program_id(0); last=pl.num_programs(0)-1
    copies=[pltpu.make_async_copy(w_hbm,w_ref,sem.at[0])]
    if t>0:
        copies.append(pltpu.make_async_copy(prev_hbm,prev_ref,sem.at[1]))
    @pl.when(f==0)
    def _():
        for z in copies:
            z.start()
    c,r=ln_stats(x_ref[0,0].astype(F32))
    xh=c*r
    n1=(xh*g_ref[...]+b_ref[...]).astype(BF)
    nd=gm_ref.shape[0]
    s_in=jnp.concatenate([gm_ref[j,0,0] for j in range(nd)],axis=0)
    dot_ref[...]=dg(wo_ref[...],s_in,1,1).astype(BF)
    n=len_ref[t]
    ks=lax.broadcasted_iota(jnp.int32,(S,1),0)
    bias=jnp.where(ks<n,0.0,-1e30)
    one=jnp.ones((S,1),F32)
    kb=lane_block([bias,one,one,one],S)
    vb=lane_block([one,one,one],S)
    oner=jnp.ones((1,S),F32)
    C=256
    units=[(h,c) for h in range(D//64) for c in range(0,S,C)]
    kts={}
    def first(n):
        h,c=units[n]; p=h//2
        kp=jnp.concatenate([k_ref[0,:,p*128:p*128+128],kb],axis=1)
        vp=jnp.concatenate([v_ref[0,:,p*128:p*128+128],vb],axis=1)
        hs=slice(h*64,h*64+64)
        do=dot_ref[hs,c:c+C]
        dd=jnp.sum(do.astype(F32)*ht_ref[0,hs,c:c+C].astype(F32),axis=0,keepdims=True)
        l3=[-z.astype(F32) for z in split3(l_ref[0,h:h+1,c:c+C])]
        d3=[-z.astype(F32) for z in split3(dd)]
        s=dg(kp,pad_head(qt_ref[0,hs,c:c+C],h%2,row_block([oner[:,:C]]+l3,C)),1,0)
        return s,dg(vp,pad_head(do,h%2,row_block(d3,C)),1,0)
    def second(n,sd):
        e=jnp.exp2(sd[0])
        return e.astype(BF),(e*sd[1]).astype(BF)
    def third(n,e,ds):
        h,c=units[n]
        hs=slice(h*64,h*64+64)
        if h//2 not in kts:
            kts[h//2]=k_ref[0,:,h//2*128:h//2*128+128].T
        dv=dg(dot_ref[hs,c:c+C],e,1,1)
        dk=dg(qt_ref[0,hs,c:c+C],ds,1,1)*LN2
        if C<S:
            if c==0:
                part[h]=(dv,dk)
            else:
                dv=dv+part[h][0]; dk=dk+part[h][1]
                if c+C<S: part[h]=(dv,dk)
        if c+C==S:
            dpt_ref[2*D+h*64:2*D+h*64+64,:]=dv.astype(BF)
            dpt_ref[D+h*64:D+h*64+64,:]=dk.astype(BF)
        dpt_ref[h*64:h*64+64,c:c+C]=(dg(kts[h//2][h%2*64:h%2*64+64],ds,1,0)*0.125).astype(BF)
    part={}
    staged(len(units),1,first,second,third)
    @pl.when(f==0)
    def _():
        for z in copies:
            z.wait()
    dn=dg(dpt_ref[...],w_ref[...],0,1)
    @pl.when(f==0)
    def _():
        vec_ref[...]=jnp.zeros_like(vec_ref)
    vec_ref[0:1]+=jnp.sum(dn*xh,axis=0,keepdims=True)
    vec_ref[1:2]+=jnp.sum(dn,axis=0,keepdims=True)
    dx_ref[0,0]=(s_in.astype(F32)+ln_back(dn,xh,r,g_ref[...])).astype(BF)
    grads=lambda i: dg(ht_ref[0],s_in,1,0) if i==3 else dg(n1,dpt_ref[i*D:i*D+D,:],0,1)
    @pl.when(f==0)
    def _():
        for i in range(4):
            acc_ref[i]=grads(i)
    @pl.when((f>0)&(f<last))
    def _():
        for i in range(4):
            acc_ref[i]+=grads(i)
    @pl.when(f==last)
    def _():
        rp=D//nd
        for i in range(4):
            if t==0:
                put_all(gr_ref,i*rp,acc_ref[i]+grads(i))
            else:
                put(mine_ref,oth_ref,len_ref[len_ref.shape[0]-1]%2,i*rp,acc_ref[i]+grads(i),prev_ref)
        if t==0:
            put_vec(vec_ref,None,gr_ref)
        else:
            put_vec(vec_ref,prev_ref,mine_ref,oth_ref)

def run_c(t, lens, x, gm, g, b, w, wo, qt, k, v, ht, l, prev=None):
    T,F,S,D=x.shape; nd=gm.shape[0]; rw=4*(D//nd)+32
    one=lambda *sh: pl.BlockSpec(sh,lambda f,s:(0,)*len(sh),pipeline_mode=pl.Buffered(1))
    con=lambda *sh: pl.BlockSpec(sh,lambda f,s:(0,)*len(sh))
    per=lambda *sh: pl.BlockSpec((1,)+sh,lambda f,s:(f,0,0))
    in_specs=[pl.BlockSpec((1,1,S,D),lambda f,s:(t,f,0,0)),
              pl.BlockSpec((nd,1,1,S//nd,D),lambda f,s:(0,0,f,0,0)),
              one(1,D),one(1,D),pl.BlockSpec(memory_space=pl.ANY),one(D,D),per(D,S),per(S,D),per(S,D),per(D,S),per(D//64,S)]
    args=[lens,x,gm,g.reshape(1,D),b.reshape(1,D),w,wo,qt,k,v,ht,l]
    sd=jax.ShapeDtypeStruct
    out_specs=[pl.BlockSpec((1,1,S,D),lambda f,s:(t,f,0,0))]
    out_shape=[sd((T,F,S,D),BF)]
    alias={}
    scratch=[pltpu.VMEM((3*D,S),BF),pltpu.VMEM((D,S),BF),pltpu.VMEM((4,D,D),F32),pltpu.VMEM((32,D),F32),pltpu.VMEM((D,3*D),BF),pltpu.SemaphoreType.DMA((2,))]
    if t==0:
        out_specs.append(con(nd,rw,D)); out_shape.append(sd((nd,rw,D),BF))
    else:
        out_specs+=[con(nd//2,rw,D)]*2; out_shape+=[sd((nd//2,rw,D),BF)]*2
        in_specs+=[pl.BlockSpec(memory_space=pl.ANY)]*2; args+=[prev[1],prev[0]]
        scratch.append(pltpu.VMEM((nd,rw,D),BF))
        alias={len(args)-1:0}
    gs=pltpu.PrefetchScalarGridSpec(num_scalar_prefetch=1,grid=(F,),in_specs=in_specs,out_specs=out_specs,
        scratch_shapes=scratch)
    return pl.pallas_call(partial(c_kernel,t),grid_spec=gs,out_shape=out_shape,input_output_aliases=alias,
        compiler_params=pltpu.CompilerParams(vmem_limit_bytes=60<<20),name="bwd_samples",
        cost_estimate=pl.CostEstimate(flops=2_000_000_000,bytes_accessed=1<<20,transcendentals=0))(*args)

def out_kernel(nt, *refs):
    ins,out_ref=refs[:nt],refs[nt]
    for t in range(nt):
        nd=ins[t].shape[0]; sl=ins[t].shape[3]
        for j in range(nd):
            out_ref[t,0,j*sl:(j+1)*sl,:]=ins[t][j,0,0]

def run_out(outs):
    nd,_,F,sl,D=outs[0].shape; T=len(outs)
    return pl.pallas_call(partial(out_kernel,T),grid=(F,),
        in_specs=[pl.BlockSpec((nd,1,1,sl,D),lambda f,k=o.shape[1]-1:(0,k,f,0,0)) for o in outs],
        out_specs=pl.BlockSpec((T,1,nd*sl,D),lambda f:(0,f,0,0)),out_shape=jax.ShapeDtypeStruct((T,F,nd*sl,D),BF),
        compiler_params=pltpu.CompilerParams(vmem_limit_bytes=40<<20),name="rows_in_order",
        cost_estimate=pl.CostEstimate(flops=0,bytes_accessed=1<<20,transcendentals=0))(*outs)

def finish_kernel(rp, fp, at_ref, *refs):
    nt=(len(refs)-16)//2
    mids,lates=refs[:nt],refs[nt:2*nt]
    up_ref,down_ref,qkv2_ref,out2_ref,qkv1_ref,out1_ref,*vec_refs,mid_s,late_s=refs[2*nt:]
    t=at_ref[0]; f=at_ref[1]; D=mid_s.shape[1]; nq=up_ref.shape[1]//D
    km=mids[0].shape[0]; kl=lates[0].shape[0]
    for r in range(nt):
        mid_s[pl.ds(pl.multiple_of((r^t)*km,8),km)]=mids[r][...].astype(F32)
        late_s[pl.ds(pl.multiple_of((r^t)*kl,8),kl)]=lates[r][...].astype(F32)
    for q in range(nq):
        up_ref[:,q*D:q*D+D]=mid_s[q*rp:q*rp+rp]
    b=nq*rp
    down_ref[...]=mid_s[b:b+fp]
    b+=fp
    for q in range(3):
        qkv2_ref[:,q*D:q*D+D]=mid_s[b+q*rp:b+q*rp+rp]
        qkv1_ref[:,q*D:q*D+D]=late_s[q*rp:q*rp+rp]
    out2_ref[...]=mid_s[b+3*rp:b+4*rp]
    out1_ref[...]=late_s[3*rp:4*rp]
    b+=4*rp
    part=lambda row,at: pltpu.roll(jnp.broadcast_to(row,(8,D)),D-at,1)[0:1]
    for ref,src,i in zip(vec_refs,(late_s,late_s,mid_s,mid_s,mid_s,mid_s,mid_s),(4*rp,4*rp+1,b,b+1,b+2,b+3,b+4)):
        ref[...]=part(src[i:i+1],f*rp)[:,0:rp]
    per=D//fp
    row=mid_s[b+5:b+6]
    for q in range(1,nq):
        row=jnp.where(f//per==q,mid_s[b+5+q:b+6+q],row)
    vec_refs[7][...]=part(row,f%per*fp)[:,0:fp]

def run_finish(t, f, mids, lates, rp, fp, FF):
    nt=len(mids); km,D=mids[0].shape; kl=lates[0].shape[0]
    v=pl.BlockSpec(memory_space=pltpu.VMEM)
    sd=lambda *s: jax.ShapeDtypeStruct(s,F32)
    o=pl.pallas_call(partial(finish_kernel,rp,fp),in_specs=[pl.BlockSpec(memory_space=pltpu.SMEM)]+[v]*(2*nt),out_specs=[v]*14,
        out_shape=[sd(rp,FF),sd(fp,D),sd(rp,3*D),sd(rp,D),sd(rp,3*D),sd(rp,D)]+[sd(1,rp)]*7+[sd(1,fp)],
        scratch_shapes=[pltpu.VMEM((nt*km,D),F32),pltpu.VMEM((nt*kl,D),F32)],
        compiler_params=pltpu.CompilerParams(vmem_limit_bytes=40<<20),name="grads_in_order",
        cost_estimate=pl.CostEstimate(flops=0,bytes_accessed=1<<20,transcendentals=0))(jnp.stack([t,f]),*mids,*lates)
    vs=[z.reshape(-1) for z in o[6:]]
    return (*o[:6],*vs[:6],vs[7],vs[6])


def phi_pair(v):
    a=jnp.abs(v)
    t=1.0/(1.0+(0.3275911*0.7071067811865476)*a)
    e=jnp.exp2(v*v*(-0.5*LOG2E))
    y=t*(0.5*0.254829592+t*(0.5*-0.284496736+t*(0.5*1.421413741+t*(0.5*-1.453152027+t*(0.5*1.061405429)))))
    y=y*e
    return jnp.where(v<0,y,1.0-y), e*0.3989422804014327

def loop(n,rolled):
    def run(f):
        if rolled and n>1:
            pl.loop(0,n)(f)
        else:
            for i in range(n):
                f(i)
    return run

def mult(v,n):
    return v if isinstance(v,int) else pl.multiple_of(v,n)

def b_kernel(t, SB, nm, cnt_ref, *refs):
    m_refs,refs=refs[:nm],refs[nm:]
    cot_ref, g2_ref, b2_ref, w_ref, wo_ref, g3_ref, b3_ref, wu_hbm, bu_ref, wd_hbm, bd_ref, *refs=refs
    nd,_,F,_,D=cot_ref.shape
    FA=nd*F; H=D//64; FF=wu_hbm.shape[1]
    if t==0:
        rows_ref,gr_hbm,*refs=refs
        gr_ref=refs[-1]; refs=refs[:-1]
        outs=((gr_ref,gr_hbm),)
    else:
        prev_hbm,gm_ref,out_ref,mine_hbm,oth_hbm,*refs=refs
        prev_ref,sem,mine_ref,oth_ref=refs[-4:]; refs=refs[:-4]
        outs=((mine_ref,mine_hbm),(oth_ref,oth_hbm))
    n2_s, n3_s, r_s, ht_s, dpt_s, act_s, gp_s, cot_s, qt_s, k_s, v_s, e_s, m_s, rl_s, dot_s, vec_s, wu_ref, wd_ref, wsem, osem=refs
    G=FA*16; NG=SB//16; R=G*NG
    i=pl.program_id(0); last=pl.num_programs(0)-1
    if t>0:
        prev=pltpu.make_async_copy(prev_hbm,prev_ref,sem)
        @pl.when(i==0)
        def _():
            prev.start()
    at=pl.multiple_of(i*R,R); rows=pl.ds(at,R)
    weights=[pltpu.make_async_copy(wu_hbm,wu_ref,wsem.at[0]),pltpu.make_async_copy(wd_hbm,wd_ref,wsem.at[1])]
    @pl.when(i==0)
    def _():
        for z in weights:
            z.start()
    split=lambda v: jnp.concatenate([v[:,g*16:g*16+16].reshape(-1,D) for g in range(NG)],axis=0)
    def join(v,ref,kind):
        for g in range(NG):
            ref[:,kind,:,g*16:g*16+16,:]=v[g*G:g*G+G].reshape(nd,F,16,D)
    if nm==1:
        m=split(m_refs[0][...].reshape(FA,SB,D).astype(F32))
    else:
        me=cnt_ref[cnt_ref.shape[0]-1]
        for r in range(nm):
            for g in range(NG):
                m_s[pl.ds(pl.multiple_of((r^me)*(F*16)+g*G,F*16),F*16)]=m_refs[r][:,g*16:g*16+16].reshape(F*16,D).astype(F32)
        m=m_s[...]
    c,r2=ln_stats(m)
    xh2=c*r2
    n2=(xh2*g2_ref[...]+b2_ref[...]).astype(BF)
    n2_s[rows,:]=n2
    qt_s[...]=(dg(w_ref[:,0:D],n2,0,1)*QS).astype(BF)
    k_s[...]=dg(n2,w_ref[:,D:2*D],1,0).astype(BF)
    v_s[...]=dg(n2,w_ref[:,2*D:3*D],1,0).astype(BF)
    n=cnt_ref[t]
    krow=lax.broadcasted_iota(jnp.int32,(G,128),0)
    lane=lax.broadcasted_iota(jnp.int32,(G,128),1)
    kb=jnp.where(lane==0,jnp.where(krow//16>=n,-1e30,0.0),jnp.where(lane-1==krow%16,-1e30,0.0)).astype(BF)
    vb=jnp.where(lane<3,1.0,0.0).astype(BF)
    qcol=lax.broadcasted_iota(jnp.int32,(128,G),1)
    sub=lax.broadcasted_iota(jnp.int32,(128,G),0)
    qa=jnp.where((sub==0)|((sub<=16)&(sub-1!=qcol%16)),1.0,0.0).astype(BF)
    ones=jnp.ones((16,G),BF)
    pair=lambda h: slice(h//2*128,h//2*128+128)
    head=lambda h: slice(h*64,h*64+64)
    def flipper(ref,gs):
        flips={}
        def flip(h):
            if h//2 not in flips:
                flips[h//2]=ref[gs,pair(h)].T
            return flips[h//2][h%2*64:h%2*64+64]
        return flip
    def group(g):
        return pl.ds(mult(g*G,G),G),pl.ds(pl.multiple_of(at+g*G,G),G)
    @loop(NG,False)
    def _(g):
        gs,ps=group(g)
        flip=flipper(v_s,gs)
        def first(h):
            return dg(jnp.concatenate([k_s[gs,pair(h)],kb],axis=1),pad_head(qt_s[head(h),gs],h%2,qa),1,0)
        def second(h,s):
            e=jnp.exp2(s-jnp.max(s,axis=0,keepdims=True)).astype(BF)
            e_s[g*H+h]=e
            return (e,)
        def third(h,e):
            o=dg(jnp.concatenate([flip(h),ones],axis=0),e,1,0)
            rl=1.0/o[64:65]
            rl_s[g,h:h+1]=rl
            ht_s[head(h),ps]=(o[:64]*rl).astype(BF)
        staged(H,2,first,second,third)
    @pl.when(i==0)
    def _():
        vec_s[...]=jnp.zeros_like(vec_s)
    m2=m+dg(ht_s[:,rows],wo_ref[...],0,0)
    c,r3=ln_stats(m2)
    xh3=c*r3
    n3=(xh3*g3_ref[...]+b3_ref[...]).astype(BF)
    n3_s[rows,:]=n3
    cot=split(cot_ref[...].reshape(FA,SB,D))
    cot_s[rows,:]=cot
    C=512
    @pl.when(i==0)
    def _():
        for z in weights:
            z.wait()
    GU=2
    @loop(FF//(C*GU),True)
    def _(o):
        cols=lambda q: pl.ds(mult((o*GU+q)*C,C),C)
        def up(q):
            return dg(n3,wu_ref[:,cols(q)],1,0)+bu_ref[:,cols(q)],dg(cot,wd_ref[cols(q),:],1,1)
        def gelu(q,pd):
            P,ph=phi_pair(pd[0])
            gp=((P+pd[0]*ph)*pd[1]).astype(BF)
            return (pd[0]*P).astype(BF),gp
        def keep(q,act,gp):
            act_s[rows,cols(q)]=act
            gp_s[rows,cols(q)]=gp
            vec_s[pl.ds(5+o*GU+q,1)]+=jnp.sum(gp.astype(F32),axis=0,keepdims=True)
        staged(GU,1,up,gelu,keep)
    out=m2+dg(act_s[rows,:],wd_ref[...],1,0)+bd_ref[...]
    out=out.astype(BF)
    if t==0:
        join(out,rows_ref,1)
    else:
        join(out,out_ref,0)
    dn3=dg(gp_s[rows,:],wu_ref[...],1,1)
    dg3=jnp.sum(dn3*xh3,axis=0,keepdims=True)
    db3=jnp.sum(dn3,axis=0,keepdims=True)
    cotf=cot.astype(F32)
    gm2=cotf+ln_back(dn3,xh3,r3,g3_ref[...])
    rr=gm2.astype(BF)
    r_s[rows,:]=rr
    dot_s[...]=dg(wo_ref[...],rr,1,1)
    @loop(NG,False)
    def _(g):
        gs,ps=group(g)
        flip=flipper(k_s,gs)
        def first(h):
            rl=rl_s[g,h:h+1]
            do=dot_s[head(h),gs]
            dd=jnp.sum(do*ht_s[head(h),ps].astype(F32),axis=0,keepdims=True)*rl
            dob=(do*rl).astype(BF)
            d3=[-z.astype(F32) for z in split3(dd)]
            return dob,dg(jnp.concatenate([v_s[gs,pair(h)],vb],axis=1),pad_head(dob,h%2,row_block(d3,G)),1,0)
        def second(h,dd):
            e=e_s[g*H+h]
            return dd[0],e,(e.astype(F32)*dd[1]).astype(BF)
        def third(h,dob,e,ds):
            dpt_s[2*D+h*64:2*D+h*64+64,ps]=dg(dob,e,1,1).astype(BF)
            dpt_s[D+h*64:D+h*64+64,ps]=(dg(qt_s[head(h),gs],ds,1,1)*LN2).astype(BF)
            dpt_s[head(h),ps]=(dg(flip(h),ds,1,0)*0.125).astype(BF)
        staged(H,2,first,second,third)
    dn2=dg(dpt_s[:,rows],w_ref[...],0,1).astype(BF).astype(F32)
    dg2=jnp.sum(dn2*xh2,axis=0,keepdims=True)
    db2=jnp.sum(dn2,axis=0,keepdims=True)
    gm=(gm2+ln_back(dn2,xh2,r2,g2_ref[...])).astype(BF)
    join(gm,rows_ref if t==0 else gm_ref,0)
    small=[dg2,db2,dg3,db3,jnp.sum(cotf,axis=0,keepdims=True)]
    for j,z in enumerate(small):
        vec_s[j:j+1]+=z
    @pl.when(i==last)
    def _():
        rp=D//nd; fp=FF//nd; nq=FF//D
        if t==0:
            emit=lambda at,acc: put_all(gr_ref,at,acc)
        else:
            prev.wait()
            core=cnt_ref[cnt_ref.shape[0]-1]%2
            emit=lambda at,acc: put(mine_ref,oth_ref,core,at,acc,prev_ref)
        base=nq*rp
        block=lambda q: pl.ds(mult(q*D,D),D)
        lines=lambda at: pl.ds(mult(at,rp),rp)
        @loop(nq,True)
        def _(q):
            emit(lines(q*rp),dg(n3_s[...],gp_s[:,block(q)],0,0))
            acc=dg(act_s[:,block(q)],cot_s[...],0,0)
            n=D//fp
            for j in range(n//2):
                even=acc[2*j*fp:(2*j+1)*fp]; odd=acc[(2*j+1)*fp:(2*j+2)*fp]
                c=q*(n//2)+j
                if t==0:
                    gr_ref[2*c,base:base+fp]=even.astype(BF)
                    gr_ref[2*c+1,base:base+fp]=odd.astype(BF)
                else:
                    even=even+prev_ref[2*c,base:base+fp].astype(F32)
                    odd=odd+prev_ref[2*c+1,base:base+fp].astype(F32)
                    mine_ref[c,base:base+fp]=jnp.where(core==0,even,odd).astype(BF)
                    oth_ref[c,base:base+fp]=jnp.where(core==0,odd,even).astype(BF)
        base2=base+fp
        first=[pltpu.make_async_copy(v.at[:,0:base2],h.at[:,0:base2],osem.at[2*k]) for k,(v,h) in enumerate(outs)]
        for z in first:
            z.start()
        @loop(3,True)
        def _(q):
            emit(lines(base2+q*rp),dg(n2_s[...],dpt_s[block(q),:],0,1))
        emit(lines(base2+3*rp),dg(ht_s[...],r_s[...],1,0))
        if t==0:
            put_vec(vec_s,None,gr_ref)
        else:
            put_vec(vec_s,prev_ref,mine_ref,oth_ref)
        rest=[pltpu.make_async_copy(v.at[:,base2:],h.at[:,base2:],osem.at[2*k+1]) for k,(v,h) in enumerate(outs)]
        for z in rest:
            z.start()
        for z in first+rest:
            z.wait()

def run_b(t, cnt, m, cot, ck, g2,b2,w,wo,g3,b3,wu,bu,wd,bd, prev=None, SB=32):
    nd,_,F,SL,D=cot.shape; FF=wu.shape[1]; R=nd*F*SB; N=nd*F*SL; G=nd*F*16
    rw=(4+FF//D)*(D//nd)+FF//nd+32
    row=lambda kinds,k: pl.BlockSpec((nd,kinds,F,SB,D),lambda i,s:(0,k,0,i,0))
    one=lambda *sh: pl.BlockSpec(sh,lambda i,s:(0,)*len(sh),pipeline_mode=pl.Buffered(1))
    hbm=pl.BlockSpec(memory_space=pl.ANY)
    r=lambda z:z.reshape(1,-1)
    sd=jax.ShapeDtypeStruct
    pieces=isinstance(m,(list,tuple))
    ms=list(m) if pieces else [m]
    in_specs=[pl.BlockSpec((F,SB,D),lambda i,s:(0,i,0))]*nd if pieces else [row(1,0)]
    in_specs+=[row(1,ck),one(1,D),one(1,D),one(D,3*D),one(D,D),one(1,D),one(1,D),hbm,one(1,FF),hbm,one(1,D)]
    args=[cnt,*ms,cot,r(g2),r(b2),w,wo,r(g3),r(b3),wu,r(bu),wd,r(bd)]
    scratch=[pltpu.VMEM((N,D),BF),pltpu.VMEM((N,D),BF),pltpu.VMEM((N,D),BF),pltpu.VMEM((D,N),BF),pltpu.VMEM((3*D,N),BF),
             pltpu.VMEM((N,FF),BF),pltpu.VMEM((N,FF),BF),pltpu.VMEM((N,D),BF),
             pltpu.VMEM((D,R),BF),pltpu.VMEM((R,D),BF),pltpu.VMEM((R,D),BF),pltpu.VMEM((D//64*(SB//16),G,G),BF),pltpu.VMEM((R,D),F32),pltpu.VMEM((SB//16,8,G),F32),pltpu.VMEM((D,R),F32),pltpu.VMEM((32,D),F32),
             pltpu.VMEM((D,FF),BF),pltpu.VMEM((FF,D),BF),pltpu.SemaphoreType.DMA((2,)),pltpu.SemaphoreType.DMA((4,))]
    if t==0:
        out_specs=[row(2,0),hbm]; out_shape=[sd((nd,2,F,SL,D),BF),sd((nd,rw,D),BF)]
        scratch.append(pltpu.VMEM((nd,rw,D),BF))
    else:
        in_specs.append(hbm); args.append(prev)
        out_specs=[row(1,0),row(1,0),hbm,hbm]
        out_shape=[sd((nd,1,F,SL,D),BF)]*2+[sd((nd//2,rw,D),BF)]*2
        scratch+=[pltpu.VMEM((nd,rw,D),BF),pltpu.SemaphoreType.DMA,pltpu.VMEM((nd//2,rw,D),BF),pltpu.VMEM((nd//2,rw,D),BF)]
    gs=pltpu.PrefetchScalarGridSpec(num_scalar_prefetch=1,grid=(SL//SB,),in_specs=in_specs,out_specs=out_specs,scratch_shapes=scratch)
    return pl.pallas_call(partial(b_kernel,t,SB,len(ms)),grid_spec=gs,out_shape=out_shape,
        compiler_params=pltpu.CompilerParams(vmem_limit_bytes=62<<20),name="middle",
        cost_estimate=pl.CostEstimate(flops=2_000_000_000,bytes_accessed=1<<20,transcendentals=0))(*args)

from jax.sharding import PartitionSpec as P


def gather_sum(pieces):
    total=pieces[0].astype(F32)
    for z in pieces[1:]:
        total=total+z.astype(F32)
    return total

def pick(a,i,axis=0):
    return lax.dynamic_index_in_dim(a,i,axis,keepdims=False)

def swap_core(mine,oth):
    n=lax.axis_size("feat")
    return [mine,lax.ppermute(oth,"feat",[(i,i^1) for i in range(n)])]

def swap_task(s):
    nt=lax.axis_size("task"); t=lax.axis_index("task")
    nz,rw,D=s.shape
    s=s.reshape(nz,nt,rw//nt,D)
    return [pick(s,t,1)]+[lax.ppermute(pick(s,t^r,1),"task",[(i,i^r) for i in range(nt)]) for r in range(1,nt)]

def swap_chips(s):
    nf=lax.axis_size("feat"); z=lax.axis_index("feat")//2
    return [pick(s,z)]+[lax.ppermute(pick(s,z^r),"feat",[(i,i^(2*r)) for i in range(nf)]) for r in range(1,nf//2)]

def halve_chips(s,bit):
    nf=lax.axis_size("feat"); b=lax.axis_index("feat")//(2*bit)%2
    s=s.reshape(s.shape[0]//2,2,*s.shape[1:])
    return [pick(s,b,1),lax.ppermute(pick(s,1-b,1),"feat",[(i,i^(2*bit)) for i in range(nf)])]

def gather_task(s):
    nt=lax.axis_size("task")
    return [s]+[lax.ppermute(s,"task",[(i,i^r) for i in range(nt)]) for r in range(1,nt)]

def total(pieces):
    return gather_sum(pieces).astype(BF)

def move(a):
    return lax.all_to_all(a,"feat",0,0)

def move_pieces(pieces):
    n=len(pieces)
    return [pieces[0]]+[lax.ppermute(pieces[r],"feat",[(i,i^r) for i in range(n)]) for r in range(1,n)]

def middle_plain(t,cnt,m,cot,g2,b2,w,wo,g3,b3,wu,bu,wd,bd):
    FA=m.shape[0]; D=m.shape[-1]; H=D//64
    mf=m.astype(F32)
    def norm(v,g,b):
        c,r=ln_stats(v)
        return c*r*g+b
    mm=lambda a,b: jnp.einsum("fsd,de->fse",a,b,preferred_element_type=F32)
    mt=lambda a,b: jnp.einsum("fse,de->fsd",a,b,preferred_element_type=F32)
    out_sum=lambda a,b: jnp.einsum("fsd,fse->de",a,b,preferred_element_type=F32).astype(BF)
    n2=norm(mf,g2,b2).astype(BF)
    q,k,v=[z[...,0,:,:] for z in jnp.split(mm(n2,w).astype(BF).reshape(m.shape[:2]+(3,H,64)),3,axis=2)]
    keep=jnp.arange(FA)<cnt[t]
    s=jnp.where(keep,jnp.einsum("qshe,kshe->shqk",q,k,preferred_element_type=F32)*0.125,-1e30)
    pr=jax.nn.softmax(s,axis=-1)
    h2=jnp.einsum("shqk,kshe->qshe",pr.astype(BF),v,preferred_element_type=F32).astype(BF).reshape(m.shape)
    m2=mf+mm(h2,wo)
    n3,back3=jax.vjp(norm,m2,g3,b3)
    n3=n3.astype(BF)
    pre=mm(n3,wu)+bu
    act,back=jax.vjp(partial(jax.nn.gelu,approximate=False),pre)
    act=act.astype(BF)
    out=(m2+mm(act,wd)+bd).astype(BF)
    gp=back(mt(cot,wd))[0].astype(BF)
    a,dg3,db3=back3(mt(gp,wu))
    gm2=cot.astype(F32)+a
    rr=gm2.astype(BF)
    do=mt(rr,wo).astype(BF).reshape(q.shape)
    dp=jnp.einsum("qshe,kshe->shqk",do,v,preferred_element_type=F32)
    ds=(pr*(dp-jnp.sum(pr*dp,axis=-1,keepdims=True))).astype(BF)
    dq=jnp.einsum("shqk,kshe->qshe",ds,k,preferred_element_type=F32)*0.125
    dk=jnp.einsum("shqk,qshe->kshe",ds,q,preferred_element_type=F32)*0.125
    dv=jnp.einsum("shqk,qshe->kshe",pr.astype(BF),do,preferred_element_type=F32)
    dpk=jnp.stack([dq,dk,dv],axis=2).reshape(m.shape[:2]+(3*D,)).astype(BF)
    _,back2=jax.vjp(norm,mf,g2,b2)
    a,dg2,db2=back2(mt(dpk,w).astype(BF).astype(F32))
    small=jnp.concatenate([jnp.stack([dg2,db2,dg3,db3,jnp.sum(cot.astype(F32),axis=(0,1))]),jnp.zeros((3,D),F32)])
    dbu=jnp.sum(gp.astype(F32),axis=(0,1))[None]
    return out,(gm2+a).astype(BF),out_sum(n2,dpk),out_sum(h2,rr),out_sum(n3,gp),out_sum(act,cot),small,dbu

def run_b_plain(t,cnt,m,cot,ck,*rest,prev=None):
    nd,_,F,SL,D=m.shape
    out,gm,dw,dwo,dwu,dwd,small,dbu=middle_plain(t,cnt,m[:,0].reshape(nd*F,SL,D),cot[:,ck].reshape(nd*F,SL,D),*rest)
    v=jnp.concatenate([small[:5],dbu.reshape(-1,D)])
    v=jnp.pad(v,((0,32-v.shape[0]),(0,0))).astype(BF)
    out=out.reshape(nd,1,F,SL,D); gm=gm.reshape(nd,1,F,SL,D)
    blocks=lambda a: a.reshape(nd,D//nd,a.shape[1]//D,D).swapaxes(1,2).reshape(nd,-1,D)
    g=jnp.concatenate([blocks(dwu),dwd.reshape(nd,-1,D),blocks(dw),blocks(dwo),jnp.broadcast_to(v[None],(nd,)+v.shape)],axis=1)
    if t==0:
        return jnp.concatenate([gm,out],axis=1),g
    g=total([g,prev]).reshape(nd//2,2,-1,D)
    core=cnt[-1]%2
    return gm,out,pick(g,core,1),pick(g,1-core,1)

def tie(*a):
    return lax.optimization_barrier(a)

def after(a,*b):
    return lax.optimization_barrier((a,)+b)[0]

def body(x,cot,lens,cnt,g1,b1,w1,wo1,g2,b2,w2,wo2,g3,b3,wu,bu,wd,bd):
    T,F,S,D=x.shape
    FF=wu.shape[1]
    nf=lax.axis_size("feat"); nt=lax.axis_size("task"); f=lax.axis_index("feat")
    sl=S//nf; rp=D//nf; fp=FF//nf; nz=nf//2
    fused=F*nf*16<=256
    me=f.astype(jnp.int32).reshape(1)
    lens=jnp.concatenate([lens,me]); cnt=jnp.concatenate([cnt,me])
    cot0=move(cot[0].reshape(F,nf,sl,D).swapaxes(0,1)[:,None])
    mid0,save0=run_a(0,lens,x,None,g1,b1,w1,wo1,nf,fused)
    mid0=move_pieces(mid0) if fused else move(mid0)
    mid1,save1=run_a(1,lens,x,cot,g1,b1,w1,wo1,nf,False)
    if fused:
        mid0,cot0,mid1,save1=tie(mid0,cot0,mid1,save1)
    mid1=move(mid1)
    rest=(g2,b2,w2,wo2,g3,b3,wu,bu,wd,bd)
    middle=run_b if fused else run_b_plain
    rows0,gr=middle(0,cnt,mid0,cot0,0,*rest)
    mid1,rows0,gr=tie(mid1,rows0,gr)
    rows0=move(rows0)
    gm1,out1,*ga=middle(1,cnt,mid1,mid1,1,*rest,prev=gr)
    rows0,gm1,ga=tie(rows0,gm1,ga)
    a=swap_core(*ga)
    gm1=move(gm1)
    a=swap_task(total(a))
    dx,gr=run_c(0,lens,x,after(rows0,a[0]),g1,b1,w1,wo1,*save0)
    gm1,dx=tie(gm1,dx)
    out1=move(after(out1,gm1))
    dx,*gc=run_c(1,lens,x,gm1,g1,b1,w1,wo1,*save1,prev=(dx,gr))
    gc,a=tie(gc,a)
    c=swap_core(*gc)
    a=halve_chips(after(total(a),gc[0]),1)
    c,out1=tie(c,out1)
    c=swap_task(total(c))
    out=run_out((rows0,after(out1,c[0])))
    a,out=tie(a,out)
    bit=2
    while bit<nz:
        a=halve_chips(total(a),bit)
        bit*=2
    a,c,out=tie(a,c,out)
    c=swap_chips(total(c))
    a,c[0]=tie(a,c[0])
    a=gather_task(total(a)[0])
    c=gather_task(total(c))
    up,down,qkv2,out2,qkv1,out1,*vs=run_finish(lax.axis_index("task").astype(jnp.int32),f.astype(jnp.int32),a,c,rp,fp,FF)
    return (out,dx,vs[0],vs[1],qkv1,out1,vs[2],vs[3],qkv2,out2,vs[4],vs[5],up,vs[6],down,vs[7])

def solution(mesh):
    rows=P("task","feat",None,None)
    mat=P("feat",None)
    return jax.shard_map(body,mesh=mesh,
        in_specs=(rows,rows,P("task"),P("task"))+(P(),)*14,
        out_specs=(rows,rows,P("feat"),P("feat"),mat,mat,P("feat"),P("feat"),mat,mat,P("feat"),P("feat"),mat,P("feat"),mat,P("feat")),
        check_vma=False)
```
